32 devices in a mesh: flow: 8 (over z, y), grp: 4 (over x, core).
Axes of the slice: x: 2, y: 2, z: 4, core: 2. Of those that a mesh axis runs over, the one named last changes fastest.
Arguments:
- velocity: float32 [3, 64, 128, 256], P(None, 'flow', 'grp'), may hold values from -6 to 6
- eddy_visc: float32 [64, 128, 256], P('flow', 'grp'), may hold values from 0.05 to 0.4
- projection: bfloat16 [125, 512], replicated, may hold values from -0.25 to 0.25
- acoustic_state: float32 [4, 125, 4096], P(None, None, ('flow', 'grp')), may hold values from -6 to 6
- route_send: int32 [32, 32, 4], P(('flow', 'grp')), may hold values from 0 to 127, as said below
- route_place: int32 [32, 128], P(('flow', 'grp')), may hold values from 0 to 127, as said below
Outputs:
- velocity_out: float32 [3, 64, 128, 256], P(None, 'flow', 'grp')
- acoustic_out: float32 [4, 125, 4096], P(None, None, ('flow', 'grp'))
The draws below stay inside these ranges and needn't reach their ends.
Inputs may be any that keep to these rules, and one draw needn't show every extreme that they name: `route_send`: row h lists, for each owner o, the local indices of home h's elements that o holds in 4 slots, -1 in an empty slot; every local element of h stands exactly once in row h; an owner holds elements of 32 home devices, all 4 slots of each filled. `route_place`: row o is a permutation of the filled slots h * 4 + k of owner o; position j of owner o holds home h's element route_send[h, o, k].
All inputs are finite; a program needn't handle non-finite values.
Results may differ from the reference program's by a relative error of at most 0.0003.
Values sent between devices are 32-bit elements; how exact they have to be, the bound alone decides.
A program may use at most 64 MiB of HBM per device.

```python
import math
import jax
import jax.numpy as jnp
import numpy as np
from jax import lax

CX = 8
CY = 32
CZ = 256
ELEM_NODES = 125
ELEM_CELLS = 512
LES_SECTIONS = 2
AC_SECTIONS = 2
NX = 64
NY = 128
DEVS = 32
ELEM_DEV = 128
ELEMS = 4096
CAP = 4
N_FLOW = 8
N_GRP = 4


def routing_tables(key):
    group_count = ELEM_DEV // CAP
    values = jnp.arange(DEVS, dtype=jnp.int32)
    ranks = jax.random.permutation(jax.random.fold_in(key, 11), DEVS).astype(jnp.int32)
    priority = jnp.where(values == 1, -3, jnp.where(values == DEVS // 2, -2, jnp.where(values == DEVS - 1, -1, ranks)))
    shifts = jnp.argsort(priority, stable=True)[:group_count].astype(jnp.int32)
    homes = jnp.arange(DEVS, dtype=jnp.int32)
    block_key = jax.random.fold_in(key, 12)
    blocks = jax.vmap(lambda home: jax.random.permutation(jax.random.fold_in(block_key, home), ELEM_DEV))(homes)
    blocks = blocks.astype(jnp.int32).reshape(DEVS, group_count, CAP)
    owners = (homes[:, None] + shifts[None, :]) % DEVS
    sending = jnp.full((DEVS, DEVS, CAP), -1, jnp.int32).at[homes[:, None], owners].set(blocks)
    sources = (homes[:, None] - shifts[None, :]) % DEVS
    slot_ids = (sources[:, :, None] * CAP + jnp.arange(CAP, dtype=jnp.int32)[None, None, :]).reshape(DEVS, ELEM_DEV)
    place_key = jax.random.fold_in(key, 13)
    orders = jax.vmap(lambda owner: jax.random.permutation(jax.random.fold_in(place_key, owner), ELEM_DEV))(homes)
    placing = jnp.take_along_axis(slot_ids, orders.astype(jnp.int32), axis=1)
    return (sending, placing.astype(jnp.int32))


def draw_route_send(key, part):
    return routing_tables(key)[0]


def draw_route_place(key, part):
    return routing_tables(key)[1]


def shard_levels(rng, shape, split, least, high):
    loudness, own = 1.0, jax.random.fold_in(rng, 6)
    for axis_at, shards_of in split:
        heights = jnp.exp(jax.random.uniform(jax.random.fold_in(own, axis_at), (shards_of,), jnp.float32, least / len(split), high / len(split)))
        loudness = loudness * jnp.repeat(heights, shape[axis_at] // shards_of).reshape([-1 if axis == axis_at else 1 for axis in range(len(shape))])
    return loudness


def gaussian(stream_key, dims, spread, most, cuts=(), kind=jnp.bfloat16):
    drawn = jax.random.normal(stream_key, dims, jnp.float32) * spread
    if len(cuts) > 0:
        drawn = shard_levels(stream_key, dims, cuts, -0.22, 0.18) * drawn
    return jnp.clip(drawn, min=-most, max=most).astype(kind)


def setup_inputs(seed: int = 0) -> dict:
    key_list = jax.random.split(jax.random.key(seed), 7)
    velocity = gaussian(key_list[0], (3, NX, NY, CZ), 1.0, 6.0, ((1, 8), (2, 4)), jnp.float32)
    eddy_visc = jnp.clip(jnp.exp(math.log(0.4) - 2.0794415 * jax.random.uniform(key_list[1], (NX, NY, CZ), jnp.float32) ** shard_levels(key_list[1], (NX, NY, CZ), ((0, 8), (1, 4)), -0.2, 0.2)), 0.05, 0.4)
    projection = gaussian(key_list[2], (ELEM_NODES, ELEM_CELLS), ELEM_CELLS ** -0.5, 0.25)
    acoustic_state = gaussian(key_list[3], (4, ELEM_NODES, ELEMS), 1.0, 6.0, ((2, 32),), jnp.float32)
    route_send = draw_route_send(jax.random.fold_in(key_list[6], 71), 0)
    route_place = draw_route_place(jax.random.fold_in(key_list[6], 71), 0)
    return {"velocity": velocity, "eddy_visc": eddy_visc, "projection": projection, "acoustic_state": acoustic_state, "route_send": route_send, "route_place": route_place}


TIME_STEP_LES = 0.15
TIME_STEP_ACOUSTIC = 0.02
GEOMETRY = 2.0
LIFT_FACTOR = 20.0

def gll_derivative():
    gll_nodes = np.array([-1.0, -math.sqrt(3.0 / 7.0), 0.0, math.sqrt(3.0 / 7.0), 1.0])
    bary_weights = np.array([1.0 / np.prod([gll_nodes[first] - gll_nodes[other] for other in range(5) if other != first]) for first in range(5)])
    matrix = np.zeros((5, 5))
    for row_id in range(5):
        for col_id in range(5):
            if row_id != col_id:
                matrix[row_id, col_id] = bary_weights[col_id] / bary_weights[row_id] / (gll_nodes[row_id] - gll_nodes[col_id])
    for row_id in range(5):
        matrix[row_id, row_id] = -matrix[row_id].sum()
    return matrix

def neighbour_slice(field, axis_id, offset):
    length = field.shape[axis_id]
    pieces = [slice(1, -1)] * 3
    pieces[axis_id] = slice(1 + offset, length - 1 + offset)
    return field[tuple(pieces)]

def central(field, axis_id):
    return 0.5 * (neighbour_slice(field, axis_id, 1) - neighbour_slice(field, axis_id, -1))

def les_terms(padded_vel, padded_visc):
    comp_x, comp_y, comp_z = (padded_vel[0], padded_vel[1], padded_vel[2])
    vort_x = central(comp_z, 1) - central(comp_y, 2)
    vort_y = central(comp_x, 2) - central(comp_z, 0)
    vort_z = central(comp_y, 0) - central(comp_x, 1)
    centre = [neighbour_slice(padded_vel[comp], 0, 0) for comp in range(3)]
    lamb = jnp.stack([vort_y * centre[2] - vort_z * centre[1], vort_z * centre[0] - vort_x * centre[2], vort_x * centre[1] - vort_y * centre[0]])
    visc_centre = neighbour_slice(padded_visc, 0, 0)
    terms = []
    for comp in range(3):
        field = padded_vel[comp]
        middle = centre[comp]
        total = jnp.zeros_like(middle)
        for axis_id in range(3):
            upper = 0.5 * (visc_centre + neighbour_slice(padded_visc, axis_id, 1))
            lower = 0.5 * (visc_centre + neighbour_slice(padded_visc, axis_id, -1))
            total = total + upper * (neighbour_slice(field, axis_id, 1) - middle) - lower * (middle - neighbour_slice(field, axis_id, -1))
        terms.append(total)
    new_vel = jnp.stack(centre) + TIME_STEP_LES * (jnp.stack(terms) - lamb)
    return (new_vel, lamb)

def project(lamb, projection):
    size_x, size_y, size_z = (lamb.shape[1], lamb.shape[2], lamb.shape[3])
    blocks = lamb.astype(jnp.bfloat16).reshape(3, size_x // 8, 8, size_y // 8, 8, size_z // 8, 8)
    blocks = blocks.transpose(2, 4, 6, 0, 1, 3, 5).reshape(512, -1)
    source = jnp.dot(projection, blocks, preferred_element_type=jnp.float32)
    source = source.reshape(125, 3, size_x // 8, size_y // 8, size_z // 8).transpose(1, 0, 2, 3, 4)
    return source.reshape(3, 5, 5, 5, size_x // 8, size_y // 8, size_z // 8)

def face_sequence(state, axis_id):
    low_face = jnp.take(state, 0, axis=1 + axis_id)
    high_face = jnp.take(state, 4, axis=1 + axis_id)
    paired = jnp.stack([low_face, high_face], axis=4 + axis_id)
    shape = list(low_face.shape)
    shape[3 + axis_id] = shape[3 + axis_id] * 2
    return paired.reshape(shape)

def face_neighbours(extended, axis_pos, count):
    other_low = lax.slice_in_dim(extended, 0, 2 * count, 2, axis_pos)
    other_high = lax.slice_in_dim(extended, 3, 2 * count + 2, 2, axis_pos)
    return (other_low, other_high)

def along(field, axis_id):
    dmat = jnp.asarray(gll_derivative(), dtype=jnp.float32)
    moved = jnp.tensordot(dmat, field, axes=([1], [axis_id]), precision=lax.Precision.HIGHEST)
    return jnp.moveaxis(moved, 0, axis_id)

def dg_rate(state, source, neighbours):
    pressure = state[0]
    rate_p = -GEOMETRY * (along(state[1], 0) + along(state[2], 1) + along(state[3], 2))
    rate_u = [-GEOMETRY * along(pressure, comp) - source[comp] for comp in range(3)]
    rate = jnp.stack([rate_p] + rate_u)
    for axis_id in range(3):
        other_low, other_high = neighbours[axis_id]
        for normal_sign, node_at, other_face in ((-1.0, 0, other_low), (1.0, 4, other_high)):
            own_face = jnp.take(state, node_at, axis=1 + axis_id)
            corr_p = LIFT_FACTOR * 0.5 * (normal_sign * (own_face[1 + axis_id] - other_face[1 + axis_id]) + (other_face[0] - own_face[0]))
            corr_u = LIFT_FACTOR * 0.5 * (other_face[1:] - own_face[1:])
            corr_u = corr_u.at[axis_id].add(LIFT_FACTOR * 0.5 * normal_sign * (own_face[0] - other_face[0]))
            correction = jnp.concatenate([corr_p[None], corr_u], axis=0)
            rate = rate.at[(slice(None),) * (1 + axis_id) + (node_at,)].add(correction)
    return rate

def reference(velocity, eddy_visc, projection, acoustic_state, route_send, route_place):
    vel = velocity
    lamb = None
    for turn in range(LES_SECTIONS):
        padded_vel = jnp.pad(vel, ((0, 0), (1, 1), (1, 1), (1, 1)))
        padded_visc = jnp.pad(eddy_visc, 1)
        vel, lamb = les_terms(padded_vel, padded_visc)
    source = project(lamb, projection)
    block_x, block_y, block_z = (CX // 8, CY // 8, CZ // 8)
    positions = jnp.arange(ELEMS, dtype=jnp.int32)
    owners = positions // ELEM_DEV
    slot_ids = route_place.reshape(-1).astype(jnp.int32)
    homes = slot_ids // CAP
    within = slot_ids % CAP
    local_block = route_send[homes, owners, within]
    home_index = (homes * ELEM_DEV + local_block).astype(jnp.int32)
    flat = acoustic_state.reshape(500, ELEMS)
    home_flat = jnp.zeros_like(flat).at[:, home_index].set(flat)
    state = home_flat.reshape(500, N_FLOW, N_GRP, block_x, block_y, block_z).transpose(0, 1, 3, 2, 4, 5)
    state = state.reshape(4, 5, 5, 5, N_FLOW * block_x, N_GRP * block_y, block_z)
    for turn in range(AC_SECTIONS):
        neighbours = []
        for axis_id in range(3):
            sequence = face_sequence(state, axis_id)
            widths = [(0, 0)] * 6
            widths[3 + axis_id] = (1, 1)
            extended = jnp.pad(sequence, widths)
            neighbours.append(face_neighbours(extended, 3 + axis_id, state.shape[4 + axis_id]))
        state = state + TIME_STEP_ACOUSTIC * dg_rate(state, source, neighbours)
    back = state.reshape(500, N_FLOW, block_x, N_GRP, block_y, block_z).transpose(0, 1, 3, 2, 4, 5).reshape(500, ELEMS)
    acoustic_out = back[:, home_index].reshape(4, 125, ELEMS)
    return (vel, acoustic_out)
```

```python
import functools
import math

import jax
import jax.numpy as jnp
import ml_dtypes
import numpy as np
from jax import lax
from jax.experimental import pallas as pl
from jax.experimental.pallas import tpu as pltpu
from jax.sharding import PartitionSpec as P

LES_SECTIONS = 2
AC_SECTIONS = 2

TIME_STEP_LES = 0.15
TIME_STEP_ACOUSTIC = 0.02
GEOMETRY = 2.0
LIFT_FACTOR = 20.0
F32 = jnp.float32
BF16 = jnp.bfloat16


def gll_derivative():
    gll_nodes = np.array([-1.0, -math.sqrt(3.0 / 7.0), 0.0, math.sqrt(3.0 / 7.0), 1.0])
    bary_weights = np.array(
        [
            1.0
            / np.prod([gll_nodes[first] - gll_nodes[other] for other in range(5) if other != first])
            for first in range(5)
        ]
    )
    matrix = np.zeros((5, 5))
    for row_id in range(5):
        for col_id in range(5):
            if row_id != col_id:
                matrix[row_id, col_id] = (
                    bary_weights[col_id]
                    / bary_weights[row_id]
                    / (gll_nodes[row_id] - gll_nodes[col_id])
                )
    for row_id in range(5):
        matrix[row_id, row_id] = -matrix[row_id].sum()
    return matrix


def operators():
    dmat = gll_derivative()
    eye = np.eye(5)
    kron = lambda a, b, c: np.kron(np.kron(a, b), c)
    derivs = [kron(dmat, eye, eye), kron(eye, dmat, eye), kron(eye, eye, dmat)]
    own = np.zeros((512, 512))
    for k in range(3):
        u = 128 * (k + 1)
        own[u : u + 125, 0:125] += -GEOMETRY * derivs[k].T
        own[0:125, u : u + 125] += -GEOMETRY * derivs[k].T
    half = 0.5 * LIFT_FACTOR
    send = np.zeros((512, 768))
    take = np.zeros((768, 512))
    for d in range(3):
        pos = [np.arange(125) // 25, np.arange(125) // 5 % 5, np.arange(125) % 5][d]
        others = [k for k in range(3) if k != d]
        faces = {-1: np.where(pos == 0)[0], 1: np.where(pos == 4)[0]}
        for sign in (-1, 1):
            for n in faces[sign]:
                own[128 * (d + 1) + n, n] += half * sign
                own[n, 128 * (d + 1) + n] += half * sign
                for c in range(4):
                    own[128 * c + n, 128 * c + n] -= half
            base = (2 * d + (sign + 1) // 2) * 128
            for i, n in enumerate(faces[sign]):
                send[n, base + i] = 1.0
                send[128 * (d + 1) + n, base + i] = sign
                for t, k in enumerate(others):
                    send[128 * (k + 1) + n, base + 25 * (t + 1) + i] = 1.0
            for i, n in enumerate(faces[sign]):
                take[base + i, n] = 1.0
                take[base + i, 128 * (d + 1) + n] = -sign
                for t, k in enumerate(others):
                    take[base + 25 * (t + 1) + i, 128 * (k + 1) + n] = 1.0
    own = own * TIME_STEP_ACOUSTIC
    high = own.astype(ml_dtypes.bfloat16)
    low = (own - high.astype(np.float64)).astype(ml_dtypes.bfloat16)
    return high, low, send.astype(ml_dtypes.bfloat16), take.astype(ml_dtypes.bfloat16)


def cell_order(by, bz):
    count = by * bz * 8
    ids = np.arange(count)
    matrix = np.zeros((count, count), ml_dtypes.bfloat16)
    matrix[ids, (ids % 8) * (by * bz) + ids // 8] = 1
    return matrix


def pieces(value, count):
    out = []
    for _ in range(count):
        part = value.astype(BF16)
        out.append(part)
        value = value - part.astype(F32)
    return out


def mm(a, b):
    return jnp.dot(a, b, preferred_element_type=F32)


def pick(onehot, value):
    a, b, c = pieces(value, 3)
    return (mm(onehot, a) + mm(onehot, b)) + mm(onehot, c)


def outgoing_rows(state_ref, place_ref, wide_ref, slots):
    count = place_ref.shape[1]
    wide_ref[...] = jnp.zeros_like(wide_ref)
    for c in range(4):
        wide_ref[c, 0:125, :] = state_ref[c]
    rows = jnp.concatenate([wide_ref[c].T for c in range(4)], axis=1)
    ids = lax.broadcasted_iota(jnp.int32, (slots, count), 0)
    onehot = jnp.where(ids == place_ref[...], 1.0, 0.0).astype(BF16)
    return pick(onehot, rows)


def home_rows(arrived, send_ref, count):
    slots = send_ref.shape[1]
    ids = lax.broadcasted_iota(jnp.int32, (count, slots), 0)
    onehot = jnp.where(ids == send_ref[...], 1.0, 0.0).astype(BF16)
    return pick(onehot, arrived)


def leaving_rows(state, send_ref):
    slots = send_ref.shape[1]
    count = state.shape[0]
    ids = lax.broadcasted_iota(jnp.int32, (count, slots), 0)
    onehot = jnp.where(ids == send_ref[...], 1.0, 0.0).T.astype(BF16)
    return pick(onehot, state)


def place_out(returned, place_ref, out_ref):
    slots = returned.shape[0]
    count = place_ref.shape[1]
    ids = lax.broadcasted_iota(jnp.int32, (slots, count), 0)
    onehot = jnp.where(ids == place_ref[...], 1.0, 0.0).T.astype(BF16)
    rows = pick(onehot, returned)
    for c in range(4):
        out_ref[c] = rows[:, 128 * c : 128 * (c + 1)].T[0:125]


def faces_out(state, send_mat_ref):
    high, low = pieces(state, 2)
    mat = send_mat_ref[...]
    return mm(high, mat) + mm(low, mat)


def advance(state, faces, x_low, x_high, y_low, y_high, source, own_ref, own_low_ref, take_ref, bz):
    count = state.shape[0]
    rows = lax.broadcasted_iota(jnp.int32, (count, 128), 0)
    part = lambda i: faces[:, 128 * i : 128 * (i + 1)]
    from_low_y = jnp.concatenate([y_low, part(3)[: count - bz]], axis=0)
    from_high_y = jnp.concatenate([part(2)[bz:], y_high], axis=0)
    from_low_z = jnp.where(rows % bz == 0, 0.0, pltpu.roll(part(5), 1, 0))
    from_high_z = jnp.where(rows % bz == bz - 1, 0.0, pltpu.roll(part(4), count - 1, 0))
    incoming = jnp.concatenate(
        [x_low, x_high, from_low_y, from_high_y, from_low_z, from_high_z], axis=1
    )
    high, low = pieces(state, 2)
    mat = own_ref[...]
    change = mm(high, mat) + (mm(high, own_low_ref[...]) + mm(low, mat))
    in_high, in_low = pieces(incoming, 2)
    lift = mm(in_high, take_ref[...]) + mm(in_low, take_ref[...])
    scale = TIME_STEP_ACOUSTIC * 0.5 * LIFT_FACTOR
    return state + (change + scale * lift) - TIME_STEP_ACOUSTIC * source


def les_plane(vel, visc):
    rows, lanes = visc[1].shape
    lane = lax.broadcasted_iota(jnp.int32, (rows, lanes), 1)

    def around(field):
        mid = field[1]
        return (
            field[0],
            field[2],
            pltpu.roll(mid, 1, 0),
            pltpu.roll(mid, rows - 1, 0),
            jnp.where(lane == 0, 0.0, pltpu.roll(mid, 1, 1)),
            jnp.where(lane == lanes - 1, 0.0, pltpu.roll(mid, lanes - 1, 1)),
        )

    weights = [0.5 * (visc[1] + w) for w in around(visc)]
    mids = [f[1] for f in vel]
    near = [around(f) for f in vel]
    d = lambda c, axis: 0.5 * (near[c][2 * axis + 1] - near[c][2 * axis])
    vort_x = d(2, 1) - d(1, 2)
    vort_y = d(0, 2) - d(2, 0)
    vort_z = d(1, 0) - d(0, 1)
    lamb = [
        vort_y * mids[2] - vort_z * mids[1],
        vort_z * mids[0] - vort_x * mids[2],
        vort_x * mids[1] - vort_y * mids[0],
    ]
    new = []
    for c in range(3):
        total = weights[0] * (near[c][0] - mids[c])
        for i in range(1, 6):
            total = total + weights[i] * (near[c][i] - mids[c])
        new.append(mids[c] + TIME_STEP_LES * (total - lamb[c]))
    return new, lamb


def les_sections(ext_ref, mid_ref, cells_ref, vel_out_ref, edges):
    planes = ext_ref.shape[1]
    rows, lanes = ext_ref.shape[2:]
    own_rows = vel_out_ref.shape[2]
    at_x0, at_x1, at_y0, at_y1 = edges
    row = lax.broadcasted_iota(jnp.int32, (rows, lanes), 0)
    below = jnp.where(at_y0, own_rows + 4, rows)
    above = jnp.where(at_y1, own_rows, own_rows + 4)
    inside = jnp.logical_or(
        row < above, jnp.logical_and(row >= own_rows + 4, row < below)
    ).astype(F32)

    def first(i, carry):
        vel = [[ext_ref[c, i + j] for j in range(3)] for c in range(3)]
        visc = [ext_ref[3, i + j] for j in range(3)]
        new, _ = les_plane(vel, visc)
        outside = jnp.logical_or(
            jnp.logical_and(at_x0, i == 0), jnp.logical_and(at_x1, i == planes - 3)
        )
        keep = inside * jnp.where(outside, 0.0, 1.0)
        for c in range(3):
            mid_ref[c, i] = new[c] * keep
        return carry

    lax.fori_loop(0, planes - 2, first, 0)

    def second(i, carry):
        vel = [[mid_ref[c, i + j] for j in range(3)] for c in range(3)]
        visc = [ext_ref[3, i + 1 + j] for j in range(3)]
        new, lamb = les_plane(vel, visc)
        at = pl.ds(pl.multiple_of(i * 8, 8), 8)
        for c in range(3):
            vel_out_ref[c, i] = new[c][0:own_rows]
            for ey in range(own_rows // 8):
                cells_ref[c, at, ey * lanes : (ey + 1) * lanes] = lamb[c][8 * ey : 8 * ey + 8]
        return carry

    lax.fori_loop(0, planes - 4, second, 0)


def source_rows(cells_ref, order_ref, proj_ref):
    count = order_ref.shape[0] // 8
    parts = [jnp.zeros((count, 128), F32)]
    for c in range(3):
        moved = mm(cells_ref[c].astype(BF16), order_ref[...]).astype(BF16)
        cells = jnp.concatenate([moved[:, count * k : count * (k + 1)] for k in range(8)], axis=0)
        parts.append(mm(proj_ref[...], cells).T)
    return jnp.concatenate(parts, axis=1)


def pre_kernel(slots, state_ref, place_ref, out_ref, wide_ref):
    out_ref[...] = outgoing_rows(state_ref, place_ref, wide_ref, slots)


def les_kernel(
    sizes, vel_ref, visc_ref, xlo_ref, xhi_ref, ylo_ref, yhi_ref, order_ref, proj_ref,
    vel_out_ref, source_ref, ext_ref, mid_ref, cells_ref,
):
    own = vel_ref.shape[2]
    own_x = vel_ref.shape[1]
    rows = ext_ref.shape[2]
    ext_ref[:, :, own:rows, :] = jnp.zeros_like(ext_ref[:, :, own:rows, :])
    ext_ref[0:3, 2 : own_x + 2, 0:own, :] = vel_ref[...]
    ext_ref[3, 2 : own_x + 2, 0:own, :] = visc_ref[...]
    ext_ref[:, 0:2, 0:own, :] = xlo_ref[...]
    ext_ref[:, own_x + 2 : own_x + 4, 0:own, :] = xhi_ref[...]
    ext_ref[:, :, own : own + 2, :] = yhi_ref[...]
    ext_ref[:, :, rows - 2 : rows, :] = ylo_ref[...]
    f, g = lax.axis_index("flow"), lax.axis_index("grp")
    edges = (f == 0, f == sizes[0] - 1, g == 0, g == sizes[1] - 1)
    les_sections(ext_ref, mid_ref, cells_ref, vel_out_ref, edges)
    source_ref[...] = source_rows(cells_ref, order_ref, proj_ref)


def home_kernel(count, arrived_ref, send_ref, mat_ref, state_ref, faces_ref):
    state = home_rows(arrived_ref[...], send_ref, count)
    state_ref[...] = state
    faces_ref[...] = faces_out(state, mat_ref)


def section_kernel(
    bz, last, state_ref, faces_ref, xl, xh, yl, yh, source_ref, own, own_low, take, mat, send_ref, *outs
):
    new = advance(
        state_ref[...], faces_ref[...], xl[...], xh[...], yl[...], yh[...],
        source_ref[...], own, own_low, take, bz,
    )
    if last:
        outs[0][...] = leaving_rows(new, send_ref)
    else:
        outs[0][...] = new
        outs[1][...] = faces_out(new, mat)


def post_kernel(returned_ref, place_ref, out_ref):
    place_out(returned_ref[...], place_ref, out_ref)


VMEM = pl.BlockSpec(memory_space=pltpu.VMEM)


def call(kernel, args, outs, scratch=()):
    return pl.pallas_call(
        kernel,
        out_shape=[jax.ShapeDtypeStruct(s, F32) for s in outs],
        in_specs=[VMEM] * len(args),
        out_specs=[VMEM] * len(outs),
        scratch_shapes=list(scratch),
        compiler_params=pltpu.CompilerParams(vmem_limit_bytes=40 * 2**20),
    )(*args)


def shift(low_send, high_send, axis):
    peers = lax.axis_size(axis)
    up = [(i, i + 1) for i in range(peers - 1)]
    down = [(j, i) for i, j in up]
    return lax.ppermute(high_send, axis, up), lax.ppermute(low_send, axis, down)


def body(velocity, eddy_visc, projection, acoustic_state, route_send, route_place):
    own_x, own_y, lanes = velocity.shape[1:]
    by, bz = own_y // 8, lanes // 8
    sizes = (lax.axis_size("flow"), lax.axis_size("grp"))
    cap = route_send.shape[2]
    count = acoustic_state.shape[2]
    devs = sizes[0] * sizes[1]
    slots = devs * cap
    own, own_low, send_mat, take = [jnp.asarray(m) for m in operators()]
    order = jnp.asarray(cell_order(by, bz))
    sending = route_send.reshape(1, slots)
    proj = projection.reshape(125, 64, 8).transpose(0, 2, 1).reshape(125, 512)
    proj = jnp.pad(proj, ((0, 3), (0, 0)))

    def swap(value):
        value = value.reshape(devs, cap, 512)
        value = lax.all_to_all(value, ("flow", "grp"), split_axis=0, concat_axis=0, tiled=True)
        return value.reshape(slots, 512)

    (out_rows,) = call(
        functools.partial(pre_kernel, slots), (acoustic_state, route_place), [(slots, 512)],
        [pltpu.VMEM((4, 128, count), F32)],
    )
    arrived = swap(out_rows)

    fields = jnp.concatenate([velocity, eddy_visc[None]], axis=0)
    xlo, xhi = shift(fields[:, :2], fields[:, -2:], "flow")
    low_y = jnp.concatenate([xlo[:, :, :2], fields[:, :, :2], xhi[:, :, :2]], axis=1)
    high_y = jnp.concatenate([xlo[:, :, -2:], fields[:, :, -2:], xhi[:, :, -2:]], axis=1)
    ylo, yhi = shift(low_y, high_y, "grp")
    vel_out, source = call(
        functools.partial(les_kernel, sizes),
        (velocity, eddy_visc, xlo, xhi, ylo, yhi, order, proj),
        [velocity.shape, (count, 512)],
        [
            pltpu.VMEM((4, own_x + 4, own_y + 8, lanes), F32),
            pltpu.VMEM((3, own_x + 2, own_y + 8, lanes), F32),
            pltpu.VMEM((3, own_x * 8, by * lanes), F32),
        ],
    )
    state, faces = call(
        functools.partial(home_kernel, count), (arrived, sending, send_mat),
        [(count, 512), (count, 768)],
    )
    for turn in range(AC_SECTIONS):
        xl, xh = shift(faces[:, 0:128], faces[:, 128:256], "flow")
        yl, yh = shift(faces[:bz, 256:384], faces[count - bz :, 384:512], "grp")
        last = turn == AC_SECTIONS - 1
        outs = [(slots, 512)] if last else [(count, 512), (count, 768)]
        result = call(
            functools.partial(section_kernel, bz, last),
            (state, faces, xl, xh, yl, yh, source, own, own_low, take, send_mat, sending), outs,
        )
        if not last:
            state, faces = result
    returned = swap(result[0])
    (acoustic_out,) = call(post_kernel, (returned, route_place), [acoustic_state.shape])
    return (vel_out, acoustic_out)


def solution(mesh):
    placed = (
        P(None, "flow", "grp", None),
        P("flow", "grp", None),
        P(),
        P(None, None, ("flow", "grp")),
        P(("flow", "grp"), None, None),
        P(("flow", "grp"), None),
    )
    return jax.shard_map(
        body,
        mesh=mesh,
        in_specs=placed,
        out_specs=(P(None, "flow", "grp", None), P(None, None, ("flow", "grp"))),
        check_vma=False,
    )
```

```python
import functools
import math

import jax
import jax.numpy as jnp
import ml_dtypes
import numpy as np
from jax import lax
from jax.experimental import pallas as pl
from jax.experimental.pallas import tpu as pltpu
from jax.sharding import PartitionSpec as P

LES_SECTIONS = 2
AC_SECTIONS = 2

TIME_STEP_LES = 0.15
TIME_STEP_ACOUSTIC = 0.02
GEOMETRY = 2.0
LIFT_FACTOR = 20.0
F32 = jnp.float32
BF16 = jnp.bfloat16


def gll_derivative():
    gll_nodes = np.array([-1.0, -math.sqrt(3.0 / 7.0), 0.0, math.sqrt(3.0 / 7.0), 1.0])
    bary_weights = np.array(
        [
            1.0
            / np.prod([gll_nodes[first] - gll_nodes[other] for other in range(5) if other != first])
            for first in range(5)
        ]
    )
    matrix = np.zeros((5, 5))
    for row_id in range(5):
        for col_id in range(5):
            if row_id != col_id:
                matrix[row_id, col_id] = (
                    bary_weights[col_id]
                    / bary_weights[row_id]
                    / (gll_nodes[row_id] - gll_nodes[col_id])
                )
    for row_id in range(5):
        matrix[row_id, row_id] = -matrix[row_id].sum()
    return matrix


def operators():
    dmat = gll_derivative()
    eye = np.eye(5)
    kron = lambda a, b, c: np.kron(np.kron(a, b), c)
    derivs = [kron(dmat, eye, eye), kron(eye, dmat, eye), kron(eye, eye, dmat)]
    own = np.zeros((512, 512))
    for k in range(3):
        u = 128 * (k + 1)
        own[u : u + 125, 0:125] += -GEOMETRY * derivs[k].T
        own[0:125, u : u + 125] += -GEOMETRY * derivs[k].T
    half = 0.5 * LIFT_FACTOR
    send = np.zeros((512, 768))
    take = np.zeros((768, 512))
    for d in range(3):
        pos = [np.arange(125) // 25, np.arange(125) // 5 % 5, np.arange(125) % 5][d]
        others = [k for k in range(3) if k != d]
        faces = {-1: np.where(pos == 0)[0], 1: np.where(pos == 4)[0]}
        for sign in (-1, 1):
            for n in faces[sign]:
                own[128 * (d + 1) + n, n] += half * sign
                own[n, 128 * (d + 1) + n] += half * sign
                for c in range(4):
                    own[128 * c + n, 128 * c + n] -= half
            base = (2 * d + (sign + 1) // 2) * 128
            for i, n in enumerate(faces[sign]):
                send[n, base + i] = 1.0
                send[128 * (d + 1) + n, base + i] = sign
                for t, k in enumerate(others):
                    send[128 * (k + 1) + n, base + 25 * (t + 1) + i] = 1.0
            for i, n in enumerate(faces[sign]):
                take[base + i, n] = 1.0
                take[base + i, 128 * (d + 1) + n] = -sign
                for t, k in enumerate(others):
                    take[base + 25 * (t + 1) + i, 128 * (k + 1) + n] = 1.0
    own = own * TIME_STEP_ACOUSTIC
    high = own.astype(ml_dtypes.bfloat16)
    low = (own - high.astype(np.float64)).astype(ml_dtypes.bfloat16)
    return high, low, send.astype(ml_dtypes.bfloat16), take.astype(ml_dtypes.bfloat16)


def cell_order(by, bz):
    count = by * bz * 8
    ids = np.arange(count)
    matrix = np.zeros((count, count), ml_dtypes.bfloat16)
    matrix[ids, (ids % 8) * (by * bz) + ids // 8] = 1
    return matrix


def pieces(value, count):
    out = []
    for _ in range(count):
        part = value.astype(BF16)
        out.append(part)
        value = value - part.astype(F32)
    return out


def mm(a, b):
    return jnp.dot(a, b, preferred_element_type=F32)


def pick(onehot, value):
    a, b, c = pieces(value, 3)
    return (mm(onehot, a) + mm(onehot, b)) + mm(onehot, c)


def slot_matrix(place_ref, devs, cap):
    count = place_ref.shape[1]
    place = place_ref[...]
    row = (place // cap) * 8 + place % cap
    ids = lax.broadcasted_iota(jnp.int32, (devs * 8, count), 0)
    return [jnp.where(ids == row + q * cap, 1.0, 0.0) for q in range(8 // cap)]


def home_matrix(send_ref, count, cap):
    slots = send_ref.shape[1]
    ids = lax.broadcasted_iota(jnp.int32, (count, slots), 0)
    part = (lax.broadcasted_iota(jnp.int32, (count, slots), 1) % 8) // cap
    hit = ids == send_ref[...]
    return [jnp.where(jnp.logical_and(hit, part == q), 1.0, 0.0) for q in range(8 // cap)]


def spread(mats, rows):
    width = rows.shape[1] // len(mats)
    stacked = jnp.concatenate([rows[:, q * width : (q + 1) * width] for q in range(len(mats))], axis=0)
    return pick(jnp.concatenate(mats, axis=1).astype(BF16), stacked)


def gather(mats, rows):
    count = mats[0].shape[0]
    both = pick(jnp.concatenate(mats, axis=0).astype(BF16), rows)
    return jnp.concatenate([both[q * count : (q + 1) * count] for q in range(len(mats))], axis=1)


def faces_out(state, mat):
    high, low = pieces(state, 2)
    return mm(high, mat) + mm(low, mat)


def advance(state, faces, x_low, x_high, y_low, y_high, source, own_mat, own_low, take_mat, bz):
    count = state.shape[0]
    rows = lax.broadcasted_iota(jnp.int32, (count, 128), 0)
    part = lambda i: faces[:, 128 * i : 128 * (i + 1)]
    from_low_y = jnp.concatenate([y_low, part(3)[: count - bz]], axis=0)
    from_high_y = jnp.concatenate([part(2)[bz:], y_high], axis=0)
    from_low_z = jnp.where(rows % bz == 0, 0.0, pltpu.roll(part(5), 1, 0))
    from_high_z = jnp.where(rows % bz == bz - 1, 0.0, pltpu.roll(part(4), count - 1, 0))
    incoming = jnp.concatenate(
        [x_low, x_high, from_low_y, from_high_y, from_low_z, from_high_z], axis=1
    )
    high, low = pieces(state, 2)
    mat = own_mat
    change = mm(high, mat) + (mm(high, own_low) + mm(low, mat))
    in_high, in_low = pieces(incoming, 2)
    lift = mm(in_high, take_mat) + mm(in_low, take_mat)
    scale = TIME_STEP_ACOUSTIC * 0.5 * LIFT_FACTOR
    return state + (change + scale * lift) - TIME_STEP_ACOUSTIC * source


def around(field):
    mid = field[1]
    rows, lanes = mid.shape
    lane = lax.broadcasted_iota(jnp.int32, (rows, lanes), 1)
    return (
        field[0],
        field[2],
        pltpu.roll(mid, 1, 0),
        pltpu.roll(mid, rows - 1, 0),
        jnp.where(lane == 0, 0.0, pltpu.roll(mid, 1, 1)),
        jnp.where(lane == lanes - 1, 0.0, pltpu.roll(mid, lanes - 1, 1)),
    )


def lamb_plane(near, mids):
    d = lambda c, axis: 0.5 * (near[c][2 * axis + 1] - near[c][2 * axis])
    vort_x = d(2, 1) - d(1, 2)
    vort_y = d(0, 2) - d(2, 0)
    vort_z = d(1, 0) - d(0, 1)
    return [
        vort_y * mids[2] - vort_z * mids[1],
        vort_z * mids[0] - vort_x * mids[2],
        vort_x * mids[1] - vort_y * mids[0],
    ]


def les_plane(vel, visc):
    weights = [0.5 * (visc[1] + w) for w in around(visc)]
    mids = [f[1] for f in vel]
    near = [around(f) for f in vel]
    lamb = lamb_plane(near, mids)
    new = []
    for c in range(3):
        total = weights[0] * (near[c][0] - mids[c])
        for i in range(1, 6):
            total = total + weights[i] * (near[c][i] - mids[c])
        new.append(mids[c] + TIME_STEP_LES * (total - lamb[c]))
    return new


def les_first(ext_ref, mid_ref, own_rows, edges):
    planes, rows, lanes = ext_ref.shape[1:]
    at_x0, at_x1, at_y0, at_y1 = edges
    row = lax.broadcasted_iota(jnp.int32, (rows, lanes), 0)
    below = jnp.where(at_y0, own_rows + 4, rows)
    above = jnp.where(at_y1, own_rows, own_rows + 4)
    inside = jnp.where(
        jnp.logical_or(row < above, jnp.logical_and(row >= own_rows + 4, row < below)), 1.0, 0.0
    )

    def step(i, carry):
        vel = [[ext_ref[c, i + j] for j in range(3)] for c in range(3)]
        new = les_plane(vel, [ext_ref[3, i + j] for j in range(3)])
        outside = jnp.logical_or(
            jnp.logical_and(at_x0, i == 0), jnp.logical_and(at_x1, i == planes - 3)
        )
        keep = inside * jnp.where(outside, 0.0, 1.0)
        for c in range(3):
            mid_ref[c, i] = new[c] * keep
        return carry

    lax.fori_loop(0, planes - 2, step, 0)


def les_lamb(mid_ref, cells_ref, own_rows):
    planes, rows, lanes = mid_ref.shape[1:]

    def step(i, carry):
        vel = [[mid_ref[c, i + j] for j in range(3)] for c in range(3)]
        lamb = lamb_plane([around(f) for f in vel], [f[1] for f in vel])
        at = pl.ds(pl.multiple_of(i * 8, 8), 8)
        for c in range(3):
            for ey in range(own_rows // 8):
                cells_ref[c, at, ey * lanes : (ey + 1) * lanes] = lamb[c][8 * ey : 8 * ey + 8]
        return carry

    lax.fori_loop(0, planes - 2, step, 0)


def les_second(ext_ref, mid_ref, vel_out_ref):
    own_rows = vel_out_ref.shape[2]

    def step(i, carry):
        vel = [[mid_ref[c, i + j] for j in range(3)] for c in range(3)]
        new = les_plane(vel, [ext_ref[3, i + 1 + j] for j in range(3)])
        for c in range(3):
            vel_out_ref[c, i] = new[c][0:own_rows]
        return carry

    lax.fori_loop(0, vel_out_ref.shape[1], step, 0)


def source_rows(cells_ref, order, proj):
    count = order.shape[0] // 8
    parts = [jnp.zeros((count, 128), F32)]
    for c in range(3):
        moved = mm(cells_ref[c].astype(BF16), order).astype(BF16)
        cells = jnp.concatenate([moved[:, count * k : count * (k + 1)] for k in range(8)], axis=0)
        parts.append(mm(proj, cells).T)
    return jnp.concatenate(parts, axis=1)


MESH = pl.DeviceIdType.MESH


def kernel(
    sizes, cap, bz,
    vel_ref, visc_ref, state_ref, place_ref, send_ref, proj_ref, *refs,
):
    consts, refs = refs[:6], refs[6:]
    (vel_out_ref, out_ref), refs = refs[:2], refs[2:]
    local, refs = refs[:6], refs[6:]
    (
        ext, mid, cells, wide, proj_rows, out_buf, in_buf, back_out, back_in,
        stage_out, stage_in, fx_out, fx_in, fy_out, fy_in,
        local_sem, a2a_send, a2a_recv, halo_send, halo_recv, face_send, face_recv,
    ) = refs
    n_flow, n_grp = sizes
    devs = n_flow * n_grp
    f, g = lax.axis_index("flow"), lax.axis_index("grp")
    me = f * n_grp + g
    edges = (f == 0, f == n_flow - 1, g == 0, g == n_grp - 1)
    own_x, own = vel_ref.shape[1:3]
    rows = ext.shape[2]
    count = place_ref.shape[1]

    barrier = pltpu.get_barrier_semaphore()

    def greet(i, carry):
        peer = lax.rem(me + i, devs)
        pl.semaphore_signal(
            barrier, inc=1, device_id=(peer // n_grp, lax.rem(peer, n_grp)), device_id_type=MESH
        )
        return carry

    lax.fori_loop(1, devs, greet, 0)

    loads = [pltpu.make_async_copy(c, l, local_sem.at[i]) for i, (c, l) in enumerate(zip(consts, local))]
    for load in loads:
        load.start()

    ext[:, :, own:rows, :] = jnp.zeros_like(ext[:, :, own:rows, :])
    ext[0:3, 2 : own_x + 2, 0:own, :] = vel_ref[...]
    ext[3, 2 : own_x + 2, 0:own, :] = visc_ref[...]

    lower = {"flow": (f - 1, g), "grp": (f, g - 1)}
    upper = {"flow": (f + 1, g), "grp": (f, g + 1)}
    has = {"flow": (f > 0, f < n_flow - 1), "grp": (g > 0, g < n_grp - 1)}

    def pair(axis, down_src, down_dst, up_src, up_dst, send, recv, s):
        down = pltpu.make_async_remote_copy(
            down_src, down_dst, send(s), recv(s), device_id=lower[axis], device_id_type=MESH
        )
        up = pltpu.make_async_remote_copy(
            up_src, up_dst, send(s + 1), recv(s + 1), device_id=upper[axis], device_id_type=MESH
        )
        has_low, has_up = has[axis]

        def start():
            pl.when(has_low)(down.start)
            pl.when(has_up)(up.start)

        def arrive():
            pl.when(has_up)(down.wait_recv)
            pl.when(has_low)(up.wait_recv)

        def sent():
            pl.when(has_low)(down.wait_send)
            pl.when(has_up)(up.wait_send)

        return start, arrive, sent

    def at_halo(ref):
        return lambda s: ref.at[s]

    x_halo = pair(
        "flow",
        ext.at[:, 2:4, 0:own, :], ext.at[:, own_x + 2 : own_x + 4, 0:own, :],
        ext.at[:, own_x : own_x + 2, 0:own, :], ext.at[:, 0:2, 0:own, :],
        at_halo(halo_send), at_halo(halo_recv), 0,
    )
    y_halo = pair(
        "grp", stage_out.at[0], stage_in.at[1], stage_out.at[1], stage_in.at[0],
        at_halo(halo_send), at_halo(halo_recv), 2,
    )
    x_face, y_face = [], []
    for t in range(AC_SECTIONS):
        sems = (lambda s, t=t: face_send.at[t, s], lambda s, t=t: face_recv.at[t, s])
        x_face.append(pair(
            "flow", fx_out.at[t, 0], fx_in.at[t, 1], fx_out.at[t, 1], fx_in.at[t, 0], *sems, 0
        ))
        y_face.append(pair(
            "grp", fy_out.at[t, 0], fy_in.at[t, 1], fy_out.at[t, 1], fy_in.at[t, 0], *sems, 2
        ))

    @pl.when(edges[0])
    def _():
        ext[:, 0:2, 0:own, :] = jnp.zeros_like(ext[:, 0:2, 0:own, :])
        fx_in[:, 0] = jnp.zeros_like(fx_in[:, 0])

    @pl.when(edges[1])
    def _():
        ext[:, own_x + 2 :, 0:own, :] = jnp.zeros_like(ext[:, own_x + 2 :, 0:own, :])
        fx_in[:, 1] = jnp.zeros_like(fx_in[:, 1])

    @pl.when(edges[2])
    def _():
        stage_in[0] = jnp.zeros_like(stage_in[0])
        fy_in[:, 0] = jnp.zeros_like(fy_in[:, 0])

    @pl.when(edges[3])
    def _():
        stage_in[1] = jnp.zeros_like(stage_in[1])
        fy_in[:, 1] = jnp.zeros_like(fy_in[:, 1])

    pl.semaphore_wait(barrier, devs - 1)
    x_halo[0]()

    def scatter(src, dst, s):
        def step(i, carry):
            peer = lax.rem(me + i, devs)
            pltpu.make_async_remote_copy(
                src.at[peer], dst.at[me], a2a_send.at[s], a2a_recv.at[s],
                device_id=(peer // n_grp, lax.rem(peer, n_grp)), device_id_type=MESH,
            ).start()
            return carry

        lax.fori_loop(1, devs, step, 0)
        dst[me] = src[me]

    def settle(src, dst, s):
        peer = lax.rem(me + 1, devs)
        return pltpu.make_async_remote_copy(
            src.at[0 : devs - 1], dst.at[0 : devs - 1], a2a_send.at[s], a2a_recv.at[s],
            device_id=(peer // n_grp, lax.rem(peer, n_grp)), device_id_type=MESH,
        )

    wide[...] = jnp.zeros_like(wide)
    for c in range(4):
        wide[c, 0:125, :] = state_ref[c]
    owned = jnp.concatenate([wide[c].T for c in range(4)], axis=1)
    by_place = slot_matrix(place_ref, devs, cap)
    out_buf[...] = spread(by_place, owned).reshape(out_buf.shape)
    scatter(out_buf, in_buf, 0)

    x_halo[1]()
    for c in range(4):
        stage_out[0, :, 2 * c : 2 * c + 2, :] = ext[c, :, 0:2, :]
        stage_out[1, :, 2 * c : 2 * c + 2, :] = ext[c, :, own - 2 : own, :]
    y_halo[0]()

    for load in loads:
        load.wait()
    order, reorder, own_mat, own_low, send_mat, take_mat = local
    proj_rows[...] = jnp.zeros_like(proj_rows)
    proj_rows[0:125, :] = mm(proj_ref[...], reorder[...])

    def send_faces(state, t):
        faces = faces_out(state, send_mat[...])
        fx_out[t, 0] = faces[:, 0:128]
        fx_out[t, 1] = faces[:, 128:256]
        fy_out[t, 0] = faces[:bz, 256:384]
        fy_out[t, 1] = faces[count - bz :, 384:512]
        x_face[t][0]()
        y_face[t][0]()
        return faces

    def take_faces(state, faces, source, t):
        x_face[t][1]()
        y_face[t][1]()
        return advance(
            state, faces, fx_in[t, 0], fx_in[t, 1], fy_in[t, 0], fy_in[t, 1], source,
            own_mat[...], own_low[...], take_mat[...], bz,
        )

    def les_ready():
        y_halo[1]()
        for c in range(4):
            ext[c, :, own : own + 2, :] = stage_in[1, :, 2 * c : 2 * c + 2, :]
            ext[c, :, rows - 2 : rows, :] = stage_in[0, :, 2 * c : 2 * c + 2, :]

    les_ready()
    les_first(ext, mid, own, edges)
    settle(out_buf, in_buf, 0).wait_recv()
    to_home = home_matrix(send_ref, count, cap)
    state = gather(to_home, in_buf[...].reshape(devs * 8, in_buf.shape[2]))
    faces = send_faces(state, 0)
    les_lamb(mid, cells, own)
    source = source_rows(cells, order[...], proj_rows[...].astype(BF16))
    for t in range(AC_SECTIONS):
        state = take_faces(state, faces, source, t)
        if t < AC_SECTIONS - 1:
            faces = send_faces(state, t + 1)

    back_out[...] = spread([m.T for m in to_home], state).reshape(back_out.shape)
    scatter(back_out, back_in, 1)
    les_second(ext, mid, vel_out_ref)
    from_home = [m.T for m in by_place]
    settle(back_out, back_in, 1).wait_recv()
    final = gather(from_home, back_in[...].reshape(devs * 8, back_in.shape[2]))
    for c in range(4):
        out_ref[c] = final[:, 128 * c : 128 * (c + 1)].T[0:125]

    settle(out_buf, in_buf, 0).wait_send()
    settle(back_out, back_in, 1).wait_send()
    x_halo[2]()
    y_halo[2]()
    for t in range(AC_SECTIONS):
        x_face[t][2]()
        y_face[t][2]()


def body(velocity, eddy_visc, projection, acoustic_state, route_send, route_place):
    own_x, own_y, lanes = velocity.shape[1:]
    by, bz = own_y // 8, lanes // 8
    sizes = (lax.axis_size("flow"), lax.axis_size("grp"))
    cap = route_send.shape[2]
    count = acoustic_state.shape[2]
    devs = sizes[0] * sizes[1]
    width = 512 * cap // 8
    ids = np.arange(512)
    reorder = np.zeros((512, 512), ml_dtypes.bfloat16)
    reorder[ids, (ids % 8) * 64 + ids // 8] = 1
    consts = [jnp.asarray(m) for m in (cell_order(by, bz), reorder, *operators())]
    sending = jnp.broadcast_to(route_send.reshape(devs, 1, cap), (devs, 8 // cap, cap))
    args = (velocity, eddy_visc, acoustic_state, route_place, sending.reshape(1, devs * 8), projection)
    vmem = pl.BlockSpec(memory_space=pltpu.VMEM)
    dma = pltpu.SemaphoreType.DMA
    chunk = pltpu.VMEM((devs, 8, width), F32)
    return tuple(pl.pallas_call(
        functools.partial(kernel, sizes, cap, bz),
        out_shape=[
            jax.ShapeDtypeStruct(velocity.shape, F32),
            jax.ShapeDtypeStruct(acoustic_state.shape, F32),
        ],
        in_specs=[vmem] * len(args) + [pl.BlockSpec(memory_space=pl.ANY)] * len(consts),
        out_specs=[vmem] * 2,
        scratch_shapes=[pltpu.VMEM(c.shape, BF16) for c in consts] + [
            pltpu.VMEM((4, own_x + 4, own_y + 8, lanes), F32),
            pltpu.VMEM((3, own_x + 2, own_y + 8, lanes), F32),
            pltpu.VMEM((3, own_x * 8, by * lanes), F32),
            pltpu.VMEM((4, 128, count), F32),
            pltpu.VMEM((128, 512), F32),
            chunk, chunk, chunk, chunk,
            pltpu.VMEM((2, own_x + 4, 8, lanes), F32),
            pltpu.VMEM((2, own_x + 4, 8, lanes), F32),
            pltpu.VMEM((AC_SECTIONS, 2, count, 128), F32),
            pltpu.VMEM((AC_SECTIONS, 2, count, 128), F32),
            pltpu.VMEM((AC_SECTIONS, 2, bz, 128), F32),
            pltpu.VMEM((AC_SECTIONS, 2, bz, 128), F32),
            dma((len(consts),)), dma((2,)), dma((2,)), dma((4,)), dma((4,)),
            dma((AC_SECTIONS, 4)), dma((AC_SECTIONS, 4)),
        ],
        compiler_params=pltpu.CompilerParams(
            collective_id=0, has_side_effects=True, vmem_limit_bytes=56 * 2**20
        ),
    )(*args, *consts))


def solution(mesh):
    placed = (
        P(None, "flow", "grp", None),
        P("flow", "grp", None),
        P(),
        P(None, None, ("flow", "grp")),
        P(("flow", "grp"), None, None),
        P(("flow", "grp"), None),
    )
    return jax.shard_map(
        body,
        mesh=mesh,
        in_specs=placed,
        out_specs=(P(None, "flow", "grp", None), P(None, None, ("flow", "grp"))),
        check_vma=False,
    )
```

```python
import functools
import math

import jax
import jax.numpy as jnp
import ml_dtypes
import numpy as np
from jax import lax
from jax.experimental import pallas as pl
from jax.experimental.pallas import tpu as pltpu
from jax.sharding import PartitionSpec as P

LES_SECTIONS = 2
AC_SECTIONS = 2

TIME_STEP_LES = 0.15
TIME_STEP_ACOUSTIC = 0.02
GEOMETRY = 2.0
LIFT_FACTOR = 20.0
F32 = jnp.float32
BF16 = jnp.bfloat16


def gll_derivative():
    gll_nodes = np.array([-1.0, -math.sqrt(3.0 / 7.0), 0.0, math.sqrt(3.0 / 7.0), 1.0])
    bary_weights = np.array(
        [
            1.0
            / np.prod([gll_nodes[first] - gll_nodes[other] for other in range(5) if other != first])
            for first in range(5)
        ]
    )
    matrix = np.zeros((5, 5))
    for row_id in range(5):
        for col_id in range(5):
            if row_id != col_id:
                matrix[row_id, col_id] = (
                    bary_weights[col_id]
                    / bary_weights[row_id]
                    / (gll_nodes[row_id] - gll_nodes[col_id])
                )
    for row_id in range(5):
        matrix[row_id, row_id] = -matrix[row_id].sum()
    return matrix


def operators():
    dmat = gll_derivative()
    eye = np.eye(5)
    kron = lambda a, b, c: np.kron(np.kron(a, b), c)
    derivs = [kron(dmat, eye, eye), kron(eye, dmat, eye), kron(eye, eye, dmat)]
    own = np.zeros((512, 512))
    for k in range(3):
        u = 128 * (k + 1)
        own[u : u + 125, 0:125] += -GEOMETRY * derivs[k].T
        own[0:125, u : u + 125] += -GEOMETRY * derivs[k].T
    half = 0.5 * LIFT_FACTOR
    send = np.zeros((512, 768))
    take = np.zeros((768, 512))
    for d in range(3):
        pos = [np.arange(125) // 25, np.arange(125) // 5 % 5, np.arange(125) % 5][d]
        others = [k for k in range(3) if k != d]
        faces = {-1: np.where(pos == 0)[0], 1: np.where(pos == 4)[0]}
        for sign in (-1, 1):
            for n in faces[sign]:
                own[128 * (d + 1) + n, n] += half * sign
                own[n, 128 * (d + 1) + n] += half * sign
                for c in range(4):
                    own[128 * c + n, 128 * c + n] -= half
            base = (2 * d + (sign + 1) // 2) * 128
            for i, n in enumerate(faces[sign]):
                send[n, base + i] = 1.0
                send[128 * (d + 1) + n, base + i] = sign
                for t, k in enumerate(others):
                    send[128 * (k + 1) + n, base + 25 * (t + 1) + i] = 1.0
            for i, n in enumerate(faces[sign]):
                take[base + i, n] = 1.0
                take[base + i, 128 * (d + 1) + n] = -sign
                for t, k in enumerate(others):
                    take[base + 25 * (t + 1) + i, 128 * (k + 1) + n] = 1.0
    own = own * TIME_STEP_ACOUSTIC
    high = own.astype(ml_dtypes.bfloat16)
    low = (own - high.astype(np.float64)).astype(ml_dtypes.bfloat16)
    return high, low, send.astype(ml_dtypes.bfloat16), take.astype(ml_dtypes.bfloat16)


def cell_order(by, bz):
    count = by * bz * 8
    ids = np.arange(count)
    matrix = np.zeros((count, count), ml_dtypes.bfloat16)
    matrix[ids, (ids % 8) * (by * bz) + ids // 8] = 1
    return matrix


def pieces(value, count):
    out = []
    for _ in range(count):
        part = value.astype(BF16)
        out.append(part)
        value = value - part.astype(F32)
    return out


def mm(a, b):
    return jnp.dot(a, b, preferred_element_type=F32)


def pick(onehot, value):
    a, b, c = pieces(value, 3)
    return (mm(onehot, a) + mm(onehot, b)) + mm(onehot, c)


def slot_matrix(place_ref, devs, cap):
    count = place_ref.shape[1]
    place = place_ref[...]
    row = (place // cap) * 8 + place % cap
    ids = lax.broadcasted_iota(jnp.int32, (devs * 8, count), 0)
    return [jnp.where(ids == row + q * cap, 1.0, 0.0) for q in range(8 // cap)]


def home_matrix(send_ref, count):
    cap, devs = send_ref.shape
    slots = devs * 8
    wide = lambda shape, dim: lax.broadcasted_iota(jnp.int32, shape, dim)
    own = wide((devs, slots), 1) // 8 == wide((devs, slots), 0)
    each = mm(send_ref[...].astype(F32).astype(BF16), jnp.where(own, 1.0, 0.0).astype(BF16))
    kept = wide((cap, slots), 1) % cap == wide((cap, slots), 0)
    sending = jnp.sum(jnp.where(kept, each, 0.0), axis=0, keepdims=True).astype(jnp.int32)
    ids = wide((count, slots), 0)
    part = (wide((count, slots), 1) % 8) // cap
    hit = ids == sending
    return [jnp.where(jnp.logical_and(hit, part == q), 1.0, 0.0) for q in range(8 // cap)]


def spread(mats, rows):
    width = rows.shape[1] // len(mats)
    stacked = jnp.concatenate([rows[:, q * width : (q + 1) * width] for q in range(len(mats))], axis=0)
    return pick(jnp.concatenate(mats, axis=1).astype(BF16), stacked)


def gather(mats, rows):
    count = mats[0].shape[0]
    both = pick(jnp.concatenate(mats, axis=0).astype(BF16), rows)
    return jnp.concatenate([both[q * count : (q + 1) * count] for q in range(len(mats))], axis=1)


def faces_out(state, mat):
    high, low = pieces(state, 2)
    return mm(high, mat) + mm(low, mat)


def advance(state, faces, x_low, x_high, y_low, y_high, source, own_mat, own_low, take_mat, bz):
    count = state.shape[0]
    rows = lax.broadcasted_iota(jnp.int32, (count, 128), 0)
    part = lambda i: faces[:, 128 * i : 128 * (i + 1)]
    from_low_y = jnp.concatenate([y_low, part(3)[: count - bz]], axis=0)
    from_high_y = jnp.concatenate([part(2)[bz:], y_high], axis=0)
    from_low_z = jnp.where(rows % bz == 0, 0.0, pltpu.roll(part(5), 1, 0))
    from_high_z = jnp.where(rows % bz == bz - 1, 0.0, pltpu.roll(part(4), count - 1, 0))
    incoming = jnp.concatenate(
        [x_low, x_high, from_low_y, from_high_y, from_low_z, from_high_z], axis=1
    )
    high, low = pieces(state, 2)
    mat = own_mat
    change = mm(high, mat) + (mm(high, own_low) + mm(low, mat))
    in_high, in_low = pieces(incoming, 2)
    lift = mm(in_high, take_mat) + mm(in_low, take_mat)
    scale = TIME_STEP_ACOUSTIC * 0.5 * LIFT_FACTOR
    return state + (change + scale * lift) - TIME_STEP_ACOUSTIC * source


def around(field):
    mid = field[1]
    rows, lanes = mid.shape
    lane = lax.broadcasted_iota(jnp.int32, (rows, lanes), 1)
    return (
        field[0],
        field[2],
        pltpu.roll(mid, 1, 0),
        pltpu.roll(mid, rows - 1, 0),
        jnp.where(lane == 0, 0.0, pltpu.roll(mid, 1, 1)),
        jnp.where(lane == lanes - 1, 0.0, pltpu.roll(mid, lanes - 1, 1)),
    )


def lamb_plane(near, mids):
    d = lambda c, axis: 0.5 * (near[c][2 * axis + 1] - near[c][2 * axis])
    vort_x = d(2, 1) - d(1, 2)
    vort_y = d(0, 2) - d(2, 0)
    vort_z = d(1, 0) - d(0, 1)
    return [
        vort_y * mids[2] - vort_z * mids[1],
        vort_z * mids[0] - vort_x * mids[2],
        vort_x * mids[1] - vort_y * mids[0],
    ]


def les_plane(vel, visc):
    weights = [0.5 * (visc[1] + w) for w in around(visc)]
    mids = [f[1] for f in vel]
    near = [around(f) for f in vel]
    lamb = lamb_plane(near, mids)
    new = []
    for c in range(3):
        total = weights[0] * (near[c][0] - mids[c])
        for i in range(1, 6):
            total = total + weights[i] * (near[c][i] - mids[c])
        new.append(mids[c] + TIME_STEP_LES * (total - lamb[c]))
    return new


def les_first(ext_ref, mid_ref, own_rows, edges):
    planes, rows, lanes = ext_ref.shape[1:]
    at_x0, at_x1, at_y0, at_y1 = edges
    row = lax.broadcasted_iota(jnp.int32, (rows, lanes), 0)
    below = jnp.where(at_y0, own_rows + 4, rows)
    above = jnp.where(at_y1, own_rows, own_rows + 4)
    inside = jnp.where(
        jnp.logical_or(row < above, jnp.logical_and(row >= own_rows + 4, row < below)), 1.0, 0.0
    )

    def step(i, carry):
        vel = [[ext_ref[c, i + j] for j in range(3)] for c in range(3)]
        new = les_plane(vel, [ext_ref[3, i + j] for j in range(3)])
        outside = jnp.logical_or(
            jnp.logical_and(at_x0, i == 0), jnp.logical_and(at_x1, i == planes - 3)
        )
        keep = inside * jnp.where(outside, 0.0, 1.0)
        for c in range(3):
            mid_ref[c, i] = new[c] * keep
        return carry

    lax.fori_loop(0, planes - 2, step, 0)


def les_lamb(mid_ref, cells_ref, own_rows):
    planes, rows, lanes = mid_ref.shape[1:]

    def step(i, carry):
        vel = [[mid_ref[c, i + j] for j in range(3)] for c in range(3)]
        lamb = lamb_plane([around(f) for f in vel], [f[1] for f in vel])
        at = pl.ds(pl.multiple_of(i * 8, 8), 8)
        for c in range(3):
            for ey in range(own_rows // 8):
                cells_ref[c, at, ey * lanes : (ey + 1) * lanes] = lamb[c][8 * ey : 8 * ey + 8]
        return carry

    lax.fori_loop(0, planes - 2, step, 0)


def les_second(ext_ref, mid_ref, vel_out_ref):
    own_rows = vel_out_ref.shape[2]

    def step(i, carry):
        vel = [[mid_ref[c, i + j] for j in range(3)] for c in range(3)]
        new = les_plane(vel, [ext_ref[3, i + 1 + j] for j in range(3)])
        for c in range(3):
            vel_out_ref[c, i] = new[c][0:own_rows]
        return carry

    lax.fori_loop(0, vel_out_ref.shape[1], step, 0)


def source_rows(cells_ref, order, proj):
    count = order.shape[0] // 8
    parts = [jnp.zeros((count, 128), F32)]
    for c in range(3):
        moved = mm(cells_ref[c].astype(BF16), order).astype(BF16)
        cells = jnp.concatenate([moved[:, count * k : count * (k + 1)] for k in range(8)], axis=0)
        parts.append(mm(proj, cells).T)
    return jnp.concatenate(parts, axis=1)


MESH = pl.DeviceIdType.MESH


def kernel(
    sizes, cap, bz,
    vel_ref, visc_ref, state_ref, place_ref, send_ref, proj_ref, *refs,
):
    consts, refs = refs[:6], refs[6:]
    (vel_out_ref, out_ref), refs = refs[:2], refs[2:]
    local, refs = refs[:6], refs[6:]
    (
        ext, mid, cells, wide, proj_rows, out_buf, in_buf, back_out, back_in,
        stage_out, stage_in, fx_out, fx_in, fy_out, fy_in,
        local_sem, a2a_send, a2a_recv, halo_send, halo_recv, face_send, face_recv,
    ) = refs
    n_flow, n_grp = sizes
    devs = n_flow * n_grp
    f, g = lax.axis_index("flow"), lax.axis_index("grp")
    me = f * n_grp + g
    edges = (f == 0, f == n_flow - 1, g == 0, g == n_grp - 1)
    own_x, own = vel_ref.shape[1:3]
    rows = ext.shape[2]
    count = place_ref.shape[1]

    barrier = pltpu.get_barrier_semaphore()

    def greet(i, carry):
        peer = lax.rem(me + i, devs)
        pl.semaphore_signal(
            barrier, inc=1, device_id=(peer // n_grp, lax.rem(peer, n_grp)), device_id_type=MESH
        )
        return carry

    lax.fori_loop(1, devs, greet, 0)

    loads = [pltpu.make_async_copy(c, l, local_sem.at[i]) for i, (c, l) in enumerate(zip(consts, local))]
    for load in loads:
        load.start()

    ext[:, :, own:rows, :] = jnp.zeros_like(ext[:, :, own:rows, :])
    ext[0:3, 2 : own_x + 2, 0:own, :] = vel_ref[...]
    ext[3, 2 : own_x + 2, 0:own, :] = visc_ref[...]

    lower = {"flow": (f - 1, g), "grp": (f, g - 1)}
    upper = {"flow": (f + 1, g), "grp": (f, g + 1)}
    has = {"flow": (f > 0, f < n_flow - 1), "grp": (g > 0, g < n_grp - 1)}

    def pair(axis, down_src, down_dst, up_src, up_dst, send, recv, s):
        down = pltpu.make_async_remote_copy(
            down_src, down_dst, send(s), recv(s), device_id=lower[axis], device_id_type=MESH
        )
        up = pltpu.make_async_remote_copy(
            up_src, up_dst, send(s + 1), recv(s + 1), device_id=upper[axis], device_id_type=MESH
        )
        has_low, has_up = has[axis]

        def start():
            pl.when(has_low)(down.start)
            pl.when(has_up)(up.start)

        def arrive():
            pl.when(has_up)(down.wait_recv)
            pl.when(has_low)(up.wait_recv)

        def sent():
            pl.when(has_low)(down.wait_send)
            pl.when(has_up)(up.wait_send)

        return start, arrive, sent

    def at_halo(ref):
        return lambda s: ref.at[s]

    x_halo = pair(
        "flow",
        ext.at[:, 2:4, 0:own, :], ext.at[:, own_x + 2 : own_x + 4, 0:own, :],
        ext.at[:, own_x : own_x + 2, 0:own, :], ext.at[:, 0:2, 0:own, :],
        at_halo(halo_send), at_halo(halo_recv), 0,
    )
    y_halo = pair(
        "grp", stage_out.at[0], stage_in.at[1], stage_out.at[1], stage_in.at[0],
        at_halo(halo_send), at_halo(halo_recv), 2,
    )
    x_face, y_face = [], []
    for t in range(AC_SECTIONS):
        sems = (lambda s, t=t: face_send.at[t, s], lambda s, t=t: face_recv.at[t, s])
        x_face.append(pair(
            "flow", fx_out.at[t, 0], fx_in.at[t, 1], fx_out.at[t, 1], fx_in.at[t, 0], *sems, 0
        ))
        y_face.append(pair(
            "grp", fy_out.at[t, 0], fy_in.at[t, 1], fy_out.at[t, 1], fy_in.at[t, 0], *sems, 2
        ))

    @pl.when(edges[0])
    def _():
        ext[:, 0:2, 0:own, :] = jnp.zeros_like(ext[:, 0:2, 0:own, :])
        fx_in[:, 0] = jnp.zeros_like(fx_in[:, 0])

    @pl.when(edges[1])
    def _():
        ext[:, own_x + 2 :, 0:own, :] = jnp.zeros_like(ext[:, own_x + 2 :, 0:own, :])
        fx_in[:, 1] = jnp.zeros_like(fx_in[:, 1])

    @pl.when(edges[2])
    def _():
        stage_in[0] = jnp.zeros_like(stage_in[0])
        fy_in[:, 0] = jnp.zeros_like(fy_in[:, 0])

    @pl.when(edges[3])
    def _():
        stage_in[1] = jnp.zeros_like(stage_in[1])
        fy_in[:, 1] = jnp.zeros_like(fy_in[:, 1])

    pl.semaphore_wait(barrier, devs - 1)
    x_halo[0]()

    def scatter(src, dst, s):
        def step(i, carry):
            peer = lax.rem(me + i, devs)
            pltpu.make_async_remote_copy(
                src.at[peer], dst.at[me], a2a_send.at[s], a2a_recv.at[s],
                device_id=(peer // n_grp, lax.rem(peer, n_grp)), device_id_type=MESH,
            ).start()
            return carry

        lax.fori_loop(1, devs, step, 0)
        dst[me] = src[me]

    def settle(src, dst, s):
        peer = lax.rem(me + 1, devs)
        return pltpu.make_async_remote_copy(
            src.at[0 : devs - 1], dst.at[0 : devs - 1], a2a_send.at[s], a2a_recv.at[s],
            device_id=(peer // n_grp, lax.rem(peer, n_grp)), device_id_type=MESH,
        )

    wide[...] = jnp.zeros_like(wide)
    for c in range(4):
        wide[c, 0:125, :] = state_ref[:, c, :]
    owned = jnp.concatenate([wide[c].T for c in range(4)], axis=1)
    by_place = slot_matrix(place_ref, devs, cap)
    out_buf[...] = spread(by_place, owned).reshape(out_buf.shape)
    scatter(out_buf, in_buf, 0)

    x_halo[1]()
    for c in range(4):
        stage_out[0, :, 2 * c : 2 * c + 2, :] = ext[c, :, 0:2, :]
        stage_out[1, :, 2 * c : 2 * c + 2, :] = ext[c, :, own - 2 : own, :]
    y_halo[0]()

    for load in loads:
        load.wait()
    order, reorder, own_mat, own_low, send_mat, take_mat = local
    proj_rows[...] = jnp.zeros_like(proj_rows)
    proj_rows[0:125, :] = mm(proj_ref[...], reorder[...])

    def send_faces(state, t):
        faces = faces_out(state, send_mat[...])
        fx_out[t, 0] = faces[:, 0:128]
        fx_out[t, 1] = faces[:, 128:256]
        fy_out[t, 0] = faces[:bz, 256:384]
        fy_out[t, 1] = faces[count - bz :, 384:512]
        x_face[t][0]()
        y_face[t][0]()
        return faces

    def take_faces(state, faces, source, t):
        x_face[t][1]()
        y_face[t][1]()
        return advance(
            state, faces, fx_in[t, 0], fx_in[t, 1], fy_in[t, 0], fy_in[t, 1], source,
            own_mat[...], own_low[...], take_mat[...], bz,
        )

    def les_ready():
        y_halo[1]()
        for c in range(4):
            ext[c, :, own : own + 2, :] = stage_in[1, :, 2 * c : 2 * c + 2, :]
            ext[c, :, rows - 2 : rows, :] = stage_in[0, :, 2 * c : 2 * c + 2, :]

    les_ready()
    les_first(ext, mid, own, edges)
    settle(out_buf, in_buf, 0).wait_recv()
    to_home = home_matrix(send_ref, count)
    state = gather(to_home, in_buf[...].reshape(devs * 8, in_buf.shape[2]))
    faces = send_faces(state, 0)
    les_lamb(mid, cells, own)
    source = source_rows(cells, order[...], proj_rows[...].astype(BF16))
    for t in range(AC_SECTIONS):
        state = take_faces(state, faces, source, t)
        if t < AC_SECTIONS - 1:
            faces = send_faces(state, t + 1)

    back_out[...] = spread([m.T for m in to_home], state).reshape(back_out.shape)
    scatter(back_out, back_in, 1)
    les_second(ext, mid, vel_out_ref)
    from_home = [m.T for m in by_place]
    settle(back_out, back_in, 1).wait_recv()
    final = gather(from_home, back_in[...].reshape(devs * 8, back_in.shape[2]))
    for c in range(4):
        out_ref[c] = final[:, 128 * c : 128 * (c + 1)].T

    settle(out_buf, in_buf, 0).wait_send()
    settle(back_out, back_in, 1).wait_send()
    x_halo[2]()
    y_halo[2]()
    for t in range(AC_SECTIONS):
        x_face[t][2]()
        y_face[t][2]()


def write_kernel(vel_ref, rows_ref, vel_out_ref, out_ref, sem):
    copy = pltpu.make_async_copy(vel_ref, vel_out_ref, sem)
    copy.start()
    for c in range(4):
        out_ref[:, c, :] = rows_ref[c, 0:125]
    copy.wait()


def body(velocity, eddy_visc, projection, acoustic_state, route_send, route_place):
    own_x, own_y, lanes = velocity.shape[1:]
    by, bz = own_y // 8, lanes // 8
    sizes = (lax.axis_size("flow"), lax.axis_size("grp"))
    cap = route_send.shape[2]
    count = acoustic_state.shape[2]
    devs = sizes[0] * sizes[1]
    width = 512 * cap // 8
    ids = np.arange(512)
    reorder = np.zeros((512, 512), ml_dtypes.bfloat16)
    reorder[ids, (ids % 8) * 64 + ids // 8] = 1
    consts = [jnp.asarray(m) for m in (cell_order(by, bz), reorder, *operators())]
    args = (
        velocity, eddy_visc, acoustic_state.transpose(1, 0, 2), route_place, route_send[0].T, projection
    )
    vmem = pl.BlockSpec(memory_space=pltpu.VMEM)
    dma = pltpu.SemaphoreType.DMA
    chunk = pltpu.VMEM((devs, 8, width), F32)
    vel_rows, final = pl.pallas_call(
        functools.partial(kernel, sizes, cap, bz),
        out_shape=[
            jax.ShapeDtypeStruct(velocity.shape, F32),
            jax.ShapeDtypeStruct((4, 128, count), F32),
        ],
        in_specs=[vmem] * len(args) + [pl.BlockSpec(memory_space=pl.ANY)] * len(consts),
        out_specs=[vmem] * 2,
        scratch_shapes=[pltpu.VMEM(c.shape, BF16) for c in consts] + [
            pltpu.VMEM((4, own_x + 4, own_y + 8, lanes), F32),
            pltpu.VMEM((3, own_x + 2, own_y + 8, lanes), F32),
            pltpu.VMEM((3, own_x * 8, by * lanes), F32),
            pltpu.VMEM((4, 128, count), F32),
            pltpu.VMEM((128, 512), F32),
            chunk, chunk, chunk, chunk,
            pltpu.VMEM((2, own_x + 4, 8, lanes), F32),
            pltpu.VMEM((2, own_x + 4, 8, lanes), F32),
            pltpu.VMEM((AC_SECTIONS, 2, count, 128), F32),
            pltpu.VMEM((AC_SECTIONS, 2, count, 128), F32),
            pltpu.VMEM((AC_SECTIONS, 2, bz, 128), F32),
            pltpu.VMEM((AC_SECTIONS, 2, bz, 128), F32),
            dma((len(consts),)), dma((2,)), dma((2,)), dma((4,)), dma((4,)),
            dma((AC_SECTIONS, 4)), dma((AC_SECTIONS, 4)),
        ],
        compiler_params=pltpu.CompilerParams(
            collective_id=0, has_side_effects=True, vmem_limit_bytes=56 * 2**20
        ),
    )(*args, *consts)
    vel_out, nodes = pl.pallas_call(
        write_kernel,
        out_shape=[
            jax.ShapeDtypeStruct(velocity.shape, F32),
            jax.ShapeDtypeStruct((125, 4, count), F32),
        ],
        in_specs=[vmem, vmem],
        out_specs=[pl.BlockSpec(memory_space=pl.ANY), vmem],
        scratch_shapes=[pltpu.SemaphoreType.DMA],
    )(vel_rows, final)
    return vel_out, nodes.transpose(1, 0, 2)


def solution(mesh):
    placed = (
        P(None, "flow", "grp", None),
        P("flow", "grp", None),
        P(),
        P(None, None, ("flow", "grp")),
        P(("flow", "grp"), None, None),
        P(("flow", "grp"), None),
    )
    return jax.shard_map(
        body,
        mesh=mesh,
        in_specs=placed,
        out_specs=(P(None, "flow", "grp", None), P(None, None, ("flow", "grp"))),
        check_vma=False,
    )
```

```python
import functools
import math

import jax
import jax.numpy as jnp
import ml_dtypes
import numpy as np
from jax import lax
from jax.experimental import pallas as pl
from jax.experimental.pallas import tpu as pltpu
from jax.sharding import PartitionSpec as P

LES_SECTIONS = 2
AC_SECTIONS = 2

TIME_STEP_LES = 0.15
TIME_STEP_ACOUSTIC = 0.02
GEOMETRY = 2.0
LIFT_FACTOR = 20.0
F32 = jnp.float32
BF16 = jnp.bfloat16


def gll_derivative():
    gll_nodes = np.array([-1.0, -math.sqrt(3.0 / 7.0), 0.0, math.sqrt(3.0 / 7.0), 1.0])
    bary_weights = np.array(
        [
            1.0
            / np.prod([gll_nodes[first] - gll_nodes[other] for other in range(5) if other != first])
            for first in range(5)
        ]
    )
    matrix = np.zeros((5, 5))
    for row_id in range(5):
        for col_id in range(5):
            if row_id != col_id:
                matrix[row_id, col_id] = (
                    bary_weights[col_id]
                    / bary_weights[row_id]
                    / (gll_nodes[row_id] - gll_nodes[col_id])
                )
    for row_id in range(5):
        matrix[row_id, row_id] = -matrix[row_id].sum()
    return matrix


def operators():
    dmat = gll_derivative()
    eye = np.eye(5)
    kron = lambda a, b, c: np.kron(np.kron(a, b), c)
    derivs = [kron(dmat, eye, eye), kron(eye, dmat, eye), kron(eye, eye, dmat)]
    own = np.zeros((512, 512))
    for k in range(3):
        u = 128 * (k + 1)
        own[u : u + 125, 0:125] += -GEOMETRY * derivs[k].T
        own[0:125, u : u + 125] += -GEOMETRY * derivs[k].T
    half = 0.5 * LIFT_FACTOR
    send = np.zeros((512, 768))
    take = np.zeros((768, 512))
    for d in range(3):
        pos = [np.arange(125) // 25, np.arange(125) // 5 % 5, np.arange(125) % 5][d]
        others = [k for k in range(3) if k != d]
        faces = {-1: np.where(pos == 0)[0], 1: np.where(pos == 4)[0]}
        for sign in (-1, 1):
            for n in faces[sign]:
                own[128 * (d + 1) + n, n] += half * sign
                own[n, 128 * (d + 1) + n] += half * sign
                for c in range(4):
                    own[128 * c + n, 128 * c + n] -= half
            base = (2 * d + (sign + 1) // 2) * 128
            for i, n in enumerate(faces[sign]):
                send[n, base + i] = 1.0
                send[128 * (d + 1) + n, base + i] = sign
                for t, k in enumerate(others):
                    send[128 * (k + 1) + n, base + 25 * (t + 1) + i] = 1.0
            for i, n in enumerate(faces[sign]):
                take[base + i, n] = 1.0
                take[base + i, 128 * (d + 1) + n] = -sign
                for t, k in enumerate(others):
                    take[base + 25 * (t + 1) + i, 128 * (k + 1) + n] = 1.0
    own = own * TIME_STEP_ACOUSTIC
    high = own.astype(ml_dtypes.bfloat16)
    low = (own - high.astype(np.float64)).astype(ml_dtypes.bfloat16)
    return high, low, send.astype(ml_dtypes.bfloat16), take.astype(ml_dtypes.bfloat16)


def cell_order(by, bz):
    count = by * bz * 8
    ids = np.arange(count)
    matrix = np.zeros((count, count), ml_dtypes.bfloat16)
    matrix[ids, (ids % 8) * (by * bz) + ids // 8] = 1
    return matrix


def pieces(value, count):
    out = []
    for _ in range(count):
        part = value.astype(BF16)
        out.append(part)
        value = value - part.astype(F32)
    return out


def mm(a, b):
    return jnp.dot(a, b, preferred_element_type=F32)


def pick(onehot, value):
    a, b, c = pieces(value, 3)
    return (mm(onehot, a) + mm(onehot, b)) + mm(onehot, c)


def slot_matrix(place_ref, devs, cap):
    count = place_ref.shape[1]
    place = place_ref[...]
    row = (place // cap) * 8 + place % cap
    ids = lax.broadcasted_iota(jnp.int32, (devs * 8, count), 0)
    return [jnp.where(ids == row + q * cap, 1.0, 0.0) for q in range(8 // cap)]


def home_matrix(send_ref, count):
    cap, devs = send_ref.shape
    slots = devs * 8
    wide = lambda shape, dim: lax.broadcasted_iota(jnp.int32, shape, dim)
    own = wide((devs, slots), 1) // 8 == wide((devs, slots), 0)
    each = mm(send_ref[...].astype(F32).astype(BF16), jnp.where(own, 1.0, 0.0).astype(BF16))
    kept = wide((cap, slots), 1) % cap == wide((cap, slots), 0)
    sending = jnp.sum(jnp.where(kept, each, 0.0), axis=0, keepdims=True).astype(jnp.int32)
    ids = wide((count, slots), 0)
    part = (wide((count, slots), 1) % 8) // cap
    hit = ids == sending
    return [jnp.where(jnp.logical_and(hit, part == q), 1.0, 0.0) for q in range(8 // cap)]


def spread(mats, rows):
    width = rows.shape[1] // len(mats)
    stacked = jnp.concatenate([rows[:, q * width : (q + 1) * width] for q in range(len(mats))], axis=0)
    return pick(jnp.concatenate(mats, axis=1).astype(BF16), stacked)


def gather(mats, rows):
    count = mats[0].shape[0]
    both = pick(jnp.concatenate(mats, axis=0).astype(BF16), rows)
    return jnp.concatenate([both[q * count : (q + 1) * count] for q in range(len(mats))], axis=1)


def faces_out(state, mat):
    high, low = pieces(state, 2)
    return mm(high, mat) + mm(low, mat)


def advance(state, faces, x_low, x_high, y_low, y_high, source, own_mat, own_low, take_mat, bz):
    count = state.shape[0]
    rows = lax.broadcasted_iota(jnp.int32, (count, 128), 0)
    part = lambda i: faces[:, 128 * i : 128 * (i + 1)]
    from_low_y = jnp.concatenate([y_low, part(3)[: count - bz]], axis=0)
    from_high_y = jnp.concatenate([part(2)[bz:], y_high], axis=0)
    from_low_z = jnp.where(rows % bz == 0, 0.0, pltpu.roll(part(5), 1, 0))
    from_high_z = jnp.where(rows % bz == bz - 1, 0.0, pltpu.roll(part(4), count - 1, 0))
    incoming = jnp.concatenate(
        [x_low, x_high, from_low_y, from_high_y, from_low_z, from_high_z], axis=1
    )
    high, low = pieces(state, 2)
    mat = own_mat
    change = mm(high, mat) + (mm(high, own_low) + mm(low, mat))
    in_high, in_low = pieces(incoming, 2)
    lift = mm(in_high, take_mat) + mm(in_low, take_mat)
    scale = TIME_STEP_ACOUSTIC * 0.5 * LIFT_FACTOR
    return state + (change + scale * lift) - TIME_STEP_ACOUSTIC * source


def around(field):
    mid = field[1]
    rows, lanes = mid.shape
    lane = lax.broadcasted_iota(jnp.int32, (rows, lanes), 1)
    return (
        field[0],
        field[2],
        pltpu.roll(mid, 1, 0),
        pltpu.roll(mid, rows - 1, 0),
        jnp.where(lane == 0, 0.0, pltpu.roll(mid, 1, 1)),
        jnp.where(lane == lanes - 1, 0.0, pltpu.roll(mid, lanes - 1, 1)),
    )


def lamb_plane(near, mids):
    d = lambda c, axis: 0.5 * (near[c][2 * axis + 1] - near[c][2 * axis])
    vort_x = d(2, 1) - d(1, 2)
    vort_y = d(0, 2) - d(2, 0)
    vort_z = d(1, 0) - d(0, 1)
    return [
        vort_y * mids[2] - vort_z * mids[1],
        vort_z * mids[0] - vort_x * mids[2],
        vort_x * mids[1] - vort_y * mids[0],
    ]


def les_plane(vel, visc):
    weights = [0.5 * (visc[1] + w) for w in around(visc)]
    mids = [f[1] for f in vel]
    near = [around(f) for f in vel]
    lamb = lamb_plane(near, mids)
    new = []
    for c in range(3):
        total = weights[0] * (near[c][0] - mids[c])
        for i in range(1, 6):
            total = total + weights[i] * (near[c][i] - mids[c])
        new.append(mids[c] + TIME_STEP_LES * (total - lamb[c]))
    return new


def les_first(ext_ref, mid_ref, own_rows, edges, spans):
    planes, rows, lanes = ext_ref.shape[1:]
    at_x0, at_x1, at_y0, at_y1 = edges
    row = lax.broadcasted_iota(jnp.int32, (rows, lanes), 0)
    below = jnp.where(at_y0, own_rows + 4, rows)
    above = jnp.where(at_y1, own_rows, own_rows + 4)
    inside = jnp.where(
        jnp.logical_or(row < above, jnp.logical_and(row >= own_rows + 4, row < below)), 1.0, 0.0
    )

    def step(i, carry):
        vel = [[ext_ref[c, i + j] for j in range(3)] for c in range(3)]
        new = les_plane(vel, [ext_ref[3, i + j] for j in range(3)])
        outside = jnp.logical_or(
            jnp.logical_and(at_x0, i == 0), jnp.logical_and(at_x1, i == planes - 3)
        )
        keep = inside * jnp.where(outside, 0.0, 1.0)
        for c in range(3):
            mid_ref[c, i] = new[c] * keep
        return carry

    for start, end in spans:
        lax.fori_loop(start, end, step, 0)


def les_lamb(mid_ref, cells_ref, own_rows):
    planes, rows, lanes = mid_ref.shape[1:]

    def step(i, carry):
        vel = [[mid_ref[c, i + j] for j in range(3)] for c in range(3)]
        lamb = lamb_plane([around(f) for f in vel], [f[1] for f in vel])
        at = pl.ds(pl.multiple_of(i * 8, 8), 8)
        for c in range(3):
            for ey in range(own_rows // 8):
                cells_ref[c, at, ey * lanes : (ey + 1) * lanes] = lamb[c][8 * ey : 8 * ey + 8]
        return carry

    lax.fori_loop(0, planes - 2, step, 0)


def les_second(ext_ref, mid_ref, vel_out_ref):
    own_rows = vel_out_ref.shape[2]

    def step(i, carry):
        vel = [[mid_ref[c, i + j] for j in range(3)] for c in range(3)]
        new = les_plane(vel, [ext_ref[3, i + 1 + j] for j in range(3)])
        for c in range(3):
            vel_out_ref[c, i] = new[c][0:own_rows]
        return carry

    lax.fori_loop(0, vel_out_ref.shape[1], step, 0)


def source_rows(cells_ref, order, proj):
    count = order.shape[0] // 8
    parts = [jnp.zeros((count, 128), F32)]
    for c in range(3):
        moved = mm(cells_ref[c].astype(BF16), order).astype(BF16)
        cells = jnp.concatenate([moved[:, count * k : count * (k + 1)] for k in range(8)], axis=0)
        parts.append(mm(proj, cells).T)
    return jnp.concatenate(parts, axis=1)


MESH = pl.DeviceIdType.MESH


def kernel(
    sizes, cap, bz,
    vel_ref, visc_ref, state_ref, place_ref, send_ref, proj_ref, *refs,
):
    consts, refs = refs[:6], refs[6:]
    (vel_out_ref, out_ref), refs = refs[:2], refs[2:]
    local, refs = refs[:6], refs[6:]
    (
        ext, mid, cells, wide, proj_rows, out_buf, in_buf, back_out, back_in,
        stage_out, stage_in, fx_out, fx_in, fy_out, fy_in,
        local_sem, a2a_send, a2a_recv, halo_send, halo_recv, face_send, face_recv,
    ) = refs
    n_flow, n_grp = sizes
    devs = n_flow * n_grp
    f, g = lax.axis_index("flow"), lax.axis_index("grp")
    me = f * n_grp + g
    edges = (f == 0, f == n_flow - 1, g == 0, g == n_grp - 1)
    own_x, own = vel_ref.shape[1:3]
    rows = ext.shape[2]
    count = place_ref.shape[1]

    barrier = pltpu.get_barrier_semaphore()

    def greet(i, carry):
        peer = lax.rem(me + i, devs)
        pl.semaphore_signal(
            barrier, inc=1, device_id=(peer // n_grp, lax.rem(peer, n_grp)), device_id_type=MESH
        )
        return carry

    lax.fori_loop(1, devs, greet, 0)

    loads = [pltpu.make_async_copy(c, l, local_sem.at[i]) for i, (c, l) in enumerate(zip(consts, local))]
    for load in loads:
        load.start()

    ext[:, :, own:rows, :] = jnp.zeros_like(ext[:, :, own:rows, :])
    ext[0:3, 2 : own_x + 2, 0:own, :] = vel_ref[...]
    ext[3, 2 : own_x + 2, 0:own, :] = visc_ref[...]

    lower = {"flow": (f - 1, g), "grp": (f, g - 1)}
    upper = {"flow": (f + 1, g), "grp": (f, g + 1)}
    has = {"flow": (f > 0, f < n_flow - 1), "grp": (g > 0, g < n_grp - 1)}

    def pair(axis, down_src, down_dst, up_src, up_dst, send, recv, s):
        down = pltpu.make_async_remote_copy(
            down_src, down_dst, send(s), recv(s), device_id=lower[axis], device_id_type=MESH
        )
        up = pltpu.make_async_remote_copy(
            up_src, up_dst, send(s + 1), recv(s + 1), device_id=upper[axis], device_id_type=MESH
        )
        has_low, has_up = has[axis]

        def start():
            pl.when(has_low)(down.start)
            pl.when(has_up)(up.start)

        def arrive():
            pl.when(has_up)(down.wait_recv)
            pl.when(has_low)(up.wait_recv)

        def sent():
            pl.when(has_low)(down.wait_send)
            pl.when(has_up)(up.wait_send)

        return start, arrive, sent

    def at_halo(ref):
        return lambda s: ref.at[s]

    x_halo = pair(
        "flow",
        ext.at[:, 2:4, 0:own, :], ext.at[:, own_x + 2 : own_x + 4, 0:own, :],
        ext.at[:, own_x : own_x + 2, 0:own, :], ext.at[:, 0:2, 0:own, :],
        at_halo(halo_send), at_halo(halo_recv), 0,
    )
    y_halo, corners = [
        pair(
            "grp", stage_out.at[0, a:b], stage_in.at[1, a:b], stage_out.at[1, a:b], stage_in.at[0, a:b],
            at_halo(halo_send), at_halo(halo_recv), s,
        )
        for a, b, s in ((0, own_x, 2), (own_x, own_x + 4, 4))
    ]
    own_planes = ((2, 0, own_x),)
    end_planes = ((0, own_x, 2), (own_x + 2, own_x + 2, 2))

    def stage(spans):
        for c in range(4):
            for at, to, n in spans:
                stage_out[0, to : to + n, 2 * c : 2 * c + 2, :] = ext[c, at : at + n, 0:2, :]
                stage_out[1, to : to + n, 2 * c : 2 * c + 2, :] = ext[c, at : at + n, own - 2 : own, :]

    def unstage(spans):
        for c in range(4):
            for at, to, n in spans:
                ext[c, at : at + n, own : own + 2, :] = stage_in[1, to : to + n, 2 * c : 2 * c + 2, :]
                ext[c, at : at + n, rows - 2 : rows, :] = stage_in[0, to : to + n, 2 * c : 2 * c + 2, :]

    x_face, y_face = [], []
    for t in range(AC_SECTIONS):
        sems = (lambda s, t=t: face_send.at[t, s], lambda s, t=t: face_recv.at[t, s])
        x_face.append(pair(
            "flow", fx_out.at[t, 0], fx_in.at[t, 1], fx_out.at[t, 1], fx_in.at[t, 0], *sems, 0
        ))
        y_face.append(pair(
            "grp", fy_out.at[t, 0], fy_in.at[t, 1], fy_out.at[t, 1], fy_in.at[t, 0], *sems, 2
        ))

    @pl.when(edges[0])
    def _():
        ext[:, 0:2, 0:own, :] = jnp.zeros_like(ext[:, 0:2, 0:own, :])
        fx_in[:, 0] = jnp.zeros_like(fx_in[:, 0])

    @pl.when(edges[1])
    def _():
        ext[:, own_x + 2 :, 0:own, :] = jnp.zeros_like(ext[:, own_x + 2 :, 0:own, :])
        fx_in[:, 1] = jnp.zeros_like(fx_in[:, 1])

    @pl.when(edges[2])
    def _():
        stage_in[0] = jnp.zeros_like(stage_in[0])
        fy_in[:, 0] = jnp.zeros_like(fy_in[:, 0])

    @pl.when(edges[3])
    def _():
        stage_in[1] = jnp.zeros_like(stage_in[1])
        fy_in[:, 1] = jnp.zeros_like(fy_in[:, 1])

    pl.semaphore_wait(barrier, devs - 1)
    x_halo[0]()
    stage(own_planes)
    y_halo[0]()

    def scatter(src, dst, s):
        def step(i, carry):
            peer = lax.rem(me + i, devs)
            pltpu.make_async_remote_copy(
                src.at[peer], dst.at[me], a2a_send.at[s], a2a_recv.at[s],
                device_id=(peer // n_grp, lax.rem(peer, n_grp)), device_id_type=MESH,
            ).start()
            return carry

        lax.fori_loop(1, devs, step, 0)
        dst[me] = src[me]

    def settle(src, dst, s):
        peer = lax.rem(me + 1, devs)
        return pltpu.make_async_remote_copy(
            src.at[0 : devs - 1], dst.at[0 : devs - 1], a2a_send.at[s], a2a_recv.at[s],
            device_id=(peer // n_grp, lax.rem(peer, n_grp)), device_id_type=MESH,
        )

    wide[...] = jnp.zeros_like(wide)
    for c in range(4):
        wide[c, 0:125, :] = state_ref[:, c, :]
    owned = jnp.concatenate([wide[c].T for c in range(4)], axis=1)
    by_place = slot_matrix(place_ref, devs, cap)
    out_buf[...] = spread(by_place, owned).reshape(out_buf.shape)
    scatter(out_buf, in_buf, 0)

    for load in loads:
        load.wait()
    order, reorder, own_mat, own_low, send_mat, take_mat = local
    proj_rows[...] = jnp.zeros_like(proj_rows)
    proj_rows[0:125, :] = mm(proj_ref[...], reorder[...])

    def send_faces(state, t):
        faces = faces_out(state, send_mat[...])
        fx_out[t, 0] = faces[:, 0:128].T[0:80]
        fx_out[t, 1] = faces[:, 128:256].T[0:80]
        fy_out[t, 0] = faces[:bz, 256:384]
        fy_out[t, 1] = faces[count - bz :, 384:512]
        x_face[t][0]()
        y_face[t][0]()
        return faces

    def face_rows(value):
        return jnp.concatenate([value, jnp.zeros((48, count), F32)], axis=0).T

    def take_faces(state, faces, source, t):
        x_face[t][1]()
        y_face[t][1]()
        return advance(
            state, faces, face_rows(fx_in[t, 0]), face_rows(fx_in[t, 1]), fy_in[t, 0], fy_in[t, 1], source,
            own_mat[...], own_low[...], take_mat[...], bz,
        )

    to_home = home_matrix(send_ref, count)
    y_halo[1]()
    unstage(own_planes)
    les_first(ext, mid, own, edges, ((2, own_x),))
    x_halo[1]()
    stage(end_planes)
    corners[0]()
    settle(out_buf, in_buf, 0).wait_recv()
    state = gather(to_home, in_buf[...].reshape(devs * 8, in_buf.shape[2]))
    faces = send_faces(state, 0)
    corners[1]()
    unstage(end_planes)
    les_first(ext, mid, own, edges, ((0, 2), (own_x, own_x + 2)))
    les_lamb(mid, cells, own)
    source = source_rows(cells, order[...], proj_rows[...].astype(BF16))
    for t in range(AC_SECTIONS):
        state = take_faces(state, faces, source, t)
        if t < AC_SECTIONS - 1:
            faces = send_faces(state, t + 1)

    back_out[...] = spread([m.T for m in to_home], state).reshape(back_out.shape)
    scatter(back_out, back_in, 1)
    les_second(ext, mid, vel_out_ref)
    from_home = [m.T for m in by_place]
    settle(back_out, back_in, 1).wait_recv()
    final = gather(from_home, back_in[...].reshape(devs * 8, back_in.shape[2]))
    for c in range(4):
        out_ref[c] = final[:, 128 * c : 128 * (c + 1)].T

    settle(out_buf, in_buf, 0).wait_send()
    settle(back_out, back_in, 1).wait_send()
    x_halo[2]()
    y_halo[2]()
    corners[2]()
    for t in range(AC_SECTIONS):
        x_face[t][2]()
        y_face[t][2]()


def write_kernel(vel_ref, rows_ref, vel_out_ref, out_ref, sem):
    copy = pltpu.make_async_copy(vel_ref, vel_out_ref, sem)
    copy.start()
    for c in range(4):
        out_ref[:, c, :] = rows_ref[c, 0:125]
    copy.wait()


def body(velocity, eddy_visc, projection, acoustic_state, route_send, route_place):
    own_x, own_y, lanes = velocity.shape[1:]
    by, bz = own_y // 8, lanes // 8
    sizes = (lax.axis_size("flow"), lax.axis_size("grp"))
    cap = route_send.shape[2]
    count = acoustic_state.shape[2]
    devs = sizes[0] * sizes[1]
    width = 512 * cap // 8
    ids = np.arange(512)
    reorder = np.zeros((512, 512), ml_dtypes.bfloat16)
    reorder[ids, (ids % 8) * 64 + ids // 8] = 1
    consts = [jnp.asarray(m) for m in (cell_order(by, bz), reorder, *operators())]
    args = (
        velocity, eddy_visc, acoustic_state.transpose(1, 0, 2), route_place, route_send[0].T, projection
    )
    vmem = pl.BlockSpec(memory_space=pltpu.VMEM)
    dma = pltpu.SemaphoreType.DMA
    chunk = pltpu.VMEM((devs, 8, width), F32)
    vel_rows, final = pl.pallas_call(
        functools.partial(kernel, sizes, cap, bz),
        out_shape=[
            jax.ShapeDtypeStruct(velocity.shape, F32),
            jax.ShapeDtypeStruct((4, 128, count), F32),
        ],
        in_specs=[vmem] * len(args) + [pl.BlockSpec(memory_space=pl.ANY)] * len(consts),
        out_specs=[vmem] * 2,
        scratch_shapes=[pltpu.VMEM(c.shape, BF16) for c in consts] + [
            pltpu.VMEM((4, own_x + 4, own_y + 8, lanes), F32),
            pltpu.VMEM((3, own_x + 2, own_y + 8, lanes), F32),
            pltpu.VMEM((3, own_x * 8, by * lanes), F32),
            pltpu.VMEM((4, 128, count), F32),
            pltpu.VMEM((128, 512), F32),
            chunk, chunk, chunk, chunk,
            pltpu.VMEM((2, own_x + 4, 8, lanes), F32),
            pltpu.VMEM((2, own_x + 4, 8, lanes), F32),
            pltpu.VMEM((AC_SECTIONS, 2, 80, count), F32),
            pltpu.VMEM((AC_SECTIONS, 2, 80, count), F32),
            pltpu.VMEM((AC_SECTIONS, 2, bz, 128), F32),
            pltpu.VMEM((AC_SECTIONS, 2, bz, 128), F32),
            dma((len(consts),)), dma((2,)), dma((2,)), dma((6,)), dma((6,)),
            dma((AC_SECTIONS, 4)), dma((AC_SECTIONS, 4)),
        ],
        compiler_params=pltpu.CompilerParams(
            collective_id=0, has_side_effects=True, vmem_limit_bytes=56 * 2**20
        ),
    )(*args, *consts)
    vel_out, nodes = pl.pallas_call(
        write_kernel,
        out_shape=[
            jax.ShapeDtypeStruct(velocity.shape, F32),
            jax.ShapeDtypeStruct((125, 4, count), F32),
        ],
        in_specs=[vmem, vmem],
        out_specs=[pl.BlockSpec(memory_space=pl.ANY), vmem],
        scratch_shapes=[pltpu.SemaphoreType.DMA],
    )(vel_rows, final)
    return vel_out, nodes.transpose(1, 0, 2)


def solution(mesh):
    placed = (
        P(None, "flow", "grp", None),
        P("flow", "grp", None),
        P(),
        P(None, None, ("flow", "grp")),
        P(("flow", "grp"), None, None),
        P(("flow", "grp"), None),
    )
    return jax.shard_map(
        body,
        mesh=mesh,
        in_specs=placed,
        out_specs=(P(None, "flow", "grp", None), P(None, None, ("flow", "grp"))),
        check_vma=False,
    )
```

```python
import functools
import math

import jax
import jax.numpy as jnp
import ml_dtypes
import numpy as np
from jax import lax
from jax.experimental import pallas as pl
from jax.experimental.pallas import tpu as pltpu
from jax.sharding import PartitionSpec as P

LES_SECTIONS = 2
AC_SECTIONS = 2

TIME_STEP_LES = 0.15
TIME_STEP_ACOUSTIC = 0.02
GEOMETRY = 2.0
LIFT_FACTOR = 20.0
F32 = jnp.float32
BF16 = jnp.bfloat16


def gll_derivative():
    gll_nodes = np.array([-1.0, -math.sqrt(3.0 / 7.0), 0.0, math.sqrt(3.0 / 7.0), 1.0])
    bary_weights = np.array(
        [
            1.0
            / np.prod([gll_nodes[first] - gll_nodes[other] for other in range(5) if other != first])
            for first in range(5)
        ]
    )
    matrix = np.zeros((5, 5))
    for row_id in range(5):
        for col_id in range(5):
            if row_id != col_id:
                matrix[row_id, col_id] = (
                    bary_weights[col_id]
                    / bary_weights[row_id]
                    / (gll_nodes[row_id] - gll_nodes[col_id])
                )
    for row_id in range(5):
        matrix[row_id, row_id] = -matrix[row_id].sum()
    return matrix


def operators():
    dmat = gll_derivative()
    eye = np.eye(5)
    kron = lambda a, b, c: np.kron(np.kron(a, b), c)
    derivs = [kron(dmat, eye, eye), kron(eye, dmat, eye), kron(eye, eye, dmat)]
    own = np.zeros((512, 512))
    for k in range(3):
        u = 128 * (k + 1)
        own[u : u + 125, 0:125] += -GEOMETRY * derivs[k].T
        own[0:125, u : u + 125] += -GEOMETRY * derivs[k].T
    half = 0.5 * LIFT_FACTOR
    send = np.zeros((512, 768))
    take = np.zeros((768, 512))
    for d in range(3):
        pos = [np.arange(125) // 25, np.arange(125) // 5 % 5, np.arange(125) % 5][d]
        others = [k for k in range(3) if k != d]
        faces = {-1: np.where(pos == 0)[0], 1: np.where(pos == 4)[0]}
        for sign in (-1, 1):
            for n in faces[sign]:
                own[128 * (d + 1) + n, n] += half * sign
                own[n, 128 * (d + 1) + n] += half * sign
                for c in range(4):
                    own[128 * c + n, 128 * c + n] -= half
            base = (2 * d + (sign + 1) // 2) * 128
            for i, n in enumerate(faces[sign]):
                send[n, base + i] = 1.0
                send[128 * (d + 1) + n, base + i] = sign
                for t, k in enumerate(others):
                    send[128 * (k + 1) + n, base + 25 * (t + 1) + i] = 1.0
            for i, n in enumerate(faces[sign]):
                take[base + i, n] = 1.0
                take[base + i, 128 * (d + 1) + n] = -sign
                for t, k in enumerate(others):
                    take[base + 25 * (t + 1) + i, 128 * (k + 1) + n] = 1.0
    own = own * TIME_STEP_ACOUSTIC
    high = own.astype(ml_dtypes.bfloat16)
    low = (own - high.astype(np.float64)).astype(ml_dtypes.bfloat16)
    return high, low, send.astype(ml_dtypes.bfloat16), take.astype(ml_dtypes.bfloat16)


def cell_order(by, bz):
    count = by * bz * 8
    ids = np.arange(count)
    matrix = np.zeros((count, count), ml_dtypes.bfloat16)
    matrix[ids, (ids % 8) * (by * bz) + ids // 8] = 1
    return matrix


def pieces(value, count):
    out = []
    for _ in range(count):
        part = value.astype(BF16)
        out.append(part)
        value = value - part.astype(F32)
    return out


def mm(a, b):
    return jnp.dot(a, b, preferred_element_type=F32)


def pick(onehot, value):
    a, b, c = pieces(value, 3)
    return (mm(onehot, a) + mm(onehot, b)) + mm(onehot, c)


def slot_matrix(place_ref, devs, cap):
    count = place_ref.shape[1]
    place = place_ref[...]
    row = (place // cap) * 8 + place % cap
    ids = lax.broadcasted_iota(jnp.int32, (devs * 8, count), 0)
    return [jnp.where(ids == row + q * cap, 1.0, 0.0) for q in range(8 // cap)]


def home_matrix(send_ref, count):
    cap, devs = send_ref.shape
    slots = devs * 8
    wide = lambda shape, dim: lax.broadcasted_iota(jnp.int32, shape, dim)
    own = wide((devs, slots), 1) // 8 == wide((devs, slots), 0)
    each = mm(send_ref[...].astype(F32).astype(BF16), jnp.where(own, 1.0, 0.0).astype(BF16))
    kept = wide((cap, slots), 1) % cap == wide((cap, slots), 0)
    sending = jnp.sum(jnp.where(kept, each, 0.0), axis=0, keepdims=True).astype(jnp.int32)
    ids = wide((count, slots), 0)
    part = (wide((count, slots), 1) % 8) // cap
    hit = ids == sending
    return [jnp.where(jnp.logical_and(hit, part == q), 1.0, 0.0) for q in range(8 // cap)]


def spread(mats, rows):
    width = rows.shape[1] // len(mats)
    stacked = jnp.concatenate([rows[:, q * width : (q + 1) * width] for q in range(len(mats))], axis=0)
    return pick(jnp.concatenate(mats, axis=1).astype(BF16), stacked)


def gather(mats, rows):
    count = mats[0].shape[0]
    both = pick(jnp.concatenate(mats, axis=0).astype(BF16), rows)
    return jnp.concatenate([both[q * count : (q + 1) * count] for q in range(len(mats))], axis=1)


def faces_out(state, mat):
    high, low = pieces(state, 2)
    return mm(high, mat) + mm(low, mat)


def own_change(state, own_mat, own_low):
    high, low = pieces(state, 2)
    return mm(high, own_mat) + (mm(high, own_low) + mm(low, own_mat))


def advance(state, faces, x_low, x_high, y_low, y_high, take_mat, bz):
    count = state.shape[0]
    rows = lax.broadcasted_iota(jnp.int32, (count, 128), 0)
    part = lambda i: faces[:, 128 * i : 128 * (i + 1)]
    from_low_y = jnp.concatenate([y_low, part(3)[: count - bz]], axis=0)
    from_high_y = jnp.concatenate([part(2)[bz:], y_high], axis=0)
    from_low_z = jnp.where(rows % bz == 0, 0.0, pltpu.roll(part(5), 1, 0))
    from_high_z = jnp.where(rows % bz == bz - 1, 0.0, pltpu.roll(part(4), count - 1, 0))
    incoming = jnp.concatenate(
        [x_low, x_high, from_low_y, from_high_y, from_low_z, from_high_z], axis=1
    )
    in_high, in_low = pieces(incoming, 2)
    lift = mm(in_high, take_mat) + mm(in_low, take_mat)
    scale = TIME_STEP_ACOUSTIC * 0.5 * LIFT_FACTOR
    return state + scale * lift


def around(field):
    mid = field[1]
    rows, lanes = mid.shape
    lane = lax.broadcasted_iota(jnp.int32, (rows, lanes), 1)
    return (
        field[0],
        field[2],
        pltpu.roll(mid, 1, 0),
        pltpu.roll(mid, rows - 1, 0),
        jnp.where(lane == 0, 0.0, pltpu.roll(mid, 1, 1)),
        jnp.where(lane == lanes - 1, 0.0, pltpu.roll(mid, lanes - 1, 1)),
    )


def lamb_plane(near, mids):
    d = lambda c, axis: 0.5 * (near[c][2 * axis + 1] - near[c][2 * axis])
    vort_x = d(2, 1) - d(1, 2)
    vort_y = d(0, 2) - d(2, 0)
    vort_z = d(1, 0) - d(0, 1)
    return [
        vort_y * mids[2] - vort_z * mids[1],
        vort_z * mids[0] - vort_x * mids[2],
        vort_x * mids[1] - vort_y * mids[0],
    ]


def les_plane(vel, visc):
    weights = [0.5 * (visc[1] + w) for w in around(visc)]
    mids = [f[1] for f in vel]
    near = [around(f) for f in vel]
    lamb = lamb_plane(near, mids)
    new = []
    for c in range(3):
        total = weights[0] * (near[c][0] - mids[c])
        for i in range(1, 6):
            total = total + weights[i] * (near[c][i] - mids[c])
        new.append(mids[c] + TIME_STEP_LES * (total - lamb[c]))
    return new


def les_first(ext_ref, mid_ref, own_rows, edges, spans):
    planes, rows, lanes = ext_ref.shape[1:]
    at_x0, at_x1, at_y0, at_y1 = edges
    row = lax.broadcasted_iota(jnp.int32, (rows, lanes), 0)
    below = jnp.where(at_y0, own_rows + 4, rows)
    above = jnp.where(at_y1, own_rows, own_rows + 4)
    inside = jnp.where(
        jnp.logical_or(row < above, jnp.logical_and(row >= own_rows + 4, row < below)), 1.0, 0.0
    )

    def step(i, carry):
        vel = [[ext_ref[c, i + j] for j in range(3)] for c in range(3)]
        new = les_plane(vel, [ext_ref[3, i + j] for j in range(3)])
        outside = jnp.logical_or(
            jnp.logical_and(at_x0, i == 0), jnp.logical_and(at_x1, i == planes - 3)
        )
        keep = inside * jnp.where(outside, 0.0, 1.0)
        for c in range(3):
            mid_ref[c, i] = new[c] * keep
        return carry

    for start, end in spans:
        lax.fori_loop(start, end, step, 0)


def les_lamb(mid_ref, cells_ref, own_rows):
    planes, rows, lanes = mid_ref.shape[1:]

    def step(i, carry):
        vel = [[mid_ref[c, i + j] for j in range(3)] for c in range(3)]
        lamb = lamb_plane([around(f) for f in vel], [f[1] for f in vel])
        at = pl.ds(pl.multiple_of(i * 8, 8), 8)
        for c in range(3):
            for ey in range(own_rows // 8):
                cells_ref[c, at, ey * lanes : (ey + 1) * lanes] = lamb[c][8 * ey : 8 * ey + 8]
        return carry

    lax.fori_loop(0, planes - 2, step, 0)


def les_second(ext_ref, mid_ref, vel_out_ref):
    own_rows = vel_out_ref.shape[2]

    def step(i, carry):
        vel = [[mid_ref[c, i + j] for j in range(3)] for c in range(3)]
        new = les_plane(vel, [ext_ref[3, i + 1 + j] for j in range(3)])
        for c in range(3):
            vel_out_ref[c, i] = new[c][0:own_rows]
        return carry

    lax.fori_loop(0, vel_out_ref.shape[1], step, 0)


def source_rows(cells_ref, order, proj):
    count = order.shape[0] // 8
    parts = [jnp.zeros((count, 128), F32)]
    for c in range(3):
        moved = mm(cells_ref[c].astype(BF16), order).astype(BF16)
        cells = jnp.concatenate([moved[:, count * k : count * (k + 1)] for k in range(8)], axis=0)
        parts.append(mm(proj, cells).T)
    return jnp.concatenate(parts, axis=1)


MESH = pl.DeviceIdType.MESH


def kernel(
    sizes, cap, bz,
    vel_ref, visc_ref, state_ref, place_ref, send_ref, proj_ref, *refs,
):
    consts, refs = refs[:6], refs[6:]
    (vel_out_ref, out_ref), refs = refs[:2], refs[2:]
    local, refs = refs[:6], refs[6:]
    (
        ext, mid, cells, wide, proj_rows, out_buf, in_buf, back_out, back_in,
        stage_out, stage_in, fx_out, fx_in, fy_out, fy_in,
        local_sem, a2a_send, a2a_recv, halo_send, halo_recv, face_send, face_recv,
    ) = refs
    n_flow, n_grp = sizes
    devs = n_flow * n_grp
    f, g = lax.axis_index("flow"), lax.axis_index("grp")
    me = f * n_grp + g
    edges = (f == 0, f == n_flow - 1, g == 0, g == n_grp - 1)
    own_x, own = vel_ref.shape[1:3]
    rows = ext.shape[2]
    count = place_ref.shape[1]

    barrier = pltpu.get_barrier_semaphore()

    def greet(i, carry):
        peer = lax.rem(me + i, devs)
        pl.semaphore_signal(
            barrier, inc=1, device_id=(peer // n_grp, lax.rem(peer, n_grp)), device_id_type=MESH
        )
        return carry

    lax.fori_loop(1, devs, greet, 0)

    loads = [pltpu.make_async_copy(c, l, local_sem.at[i]) for i, (c, l) in enumerate(zip(consts, local))]
    for load in loads:
        load.start()

    ext[:, :, own:rows, :] = jnp.zeros_like(ext[:, :, own:rows, :])
    ext[0:3, 2 : own_x + 2, 0:own, :] = vel_ref[...]
    ext[3, 2 : own_x + 2, 0:own, :] = visc_ref[...]

    lower = {"flow": (f - 1, g), "grp": (f, g - 1)}
    upper = {"flow": (f + 1, g), "grp": (f, g + 1)}
    has = {"flow": (f > 0, f < n_flow - 1), "grp": (g > 0, g < n_grp - 1)}

    def pair(axis, down_src, down_dst, up_src, up_dst, send, recv, s):
        down = pltpu.make_async_remote_copy(
            down_src, down_dst, send(s), recv(s), device_id=lower[axis], device_id_type=MESH
        )
        up = pltpu.make_async_remote_copy(
            up_src, up_dst, send(s + 1), recv(s + 1), device_id=upper[axis], device_id_type=MESH
        )
        has_low, has_up = has[axis]

        def start():
            pl.when(has_low)(down.start)
            pl.when(has_up)(up.start)

        def arrive():
            pl.when(has_up)(down.wait_recv)
            pl.when(has_low)(up.wait_recv)

        def sent():
            pl.when(has_low)(down.wait_send)
            pl.when(has_up)(up.wait_send)

        return start, arrive, sent

    def at_halo(ref):
        return lambda s: ref.at[s]

    x_halo = pair(
        "flow",
        ext.at[:, 2:4, 0:own, :], ext.at[:, own_x + 2 : own_x + 4, 0:own, :],
        ext.at[:, own_x : own_x + 2, 0:own, :], ext.at[:, 0:2, 0:own, :],
        at_halo(halo_send), at_halo(halo_recv), 0,
    )
    y_halo, corners = [
        pair(
            "grp", stage_out.at[0, a:b], stage_in.at[1, a:b], stage_out.at[1, a:b], stage_in.at[0, a:b],
            at_halo(halo_send), at_halo(halo_recv), s,
        )
        for a, b, s in ((0, own_x, 2), (own_x, own_x + 4, 4))
    ]
    own_planes = ((2, 0, own_x),)
    end_planes = ((0, own_x, 2), (own_x + 2, own_x + 2, 2))

    def stage(spans):
        for c in range(4):
            for at, to, n in spans:
                stage_out[0, to : to + n, 2 * c : 2 * c + 2, :] = ext[c, at : at + n, 0:2, :]
                stage_out[1, to : to + n, 2 * c : 2 * c + 2, :] = ext[c, at : at + n, own - 2 : own, :]

    def unstage(spans):
        for c in range(4):
            for at, to, n in spans:
                ext[c, at : at + n, own : own + 2, :] = stage_in[1, to : to + n, 2 * c : 2 * c + 2, :]
                ext[c, at : at + n, rows - 2 : rows, :] = stage_in[0, to : to + n, 2 * c : 2 * c + 2, :]

    x_face, y_face = [], []
    for t in range(AC_SECTIONS):
        sems = (lambda s, t=t: face_send.at[t, s], lambda s, t=t: face_recv.at[t, s])
        x_face.append(pair(
            "flow", fx_out.at[t, 0], fx_in.at[t, 1], fx_out.at[t, 1], fx_in.at[t, 0], *sems, 0
        ))
        y_face.append(pair(
            "grp", fy_out.at[t, 0], fy_in.at[t, 1], fy_out.at[t, 1], fy_in.at[t, 0], *sems, 2
        ))

    @pl.when(edges[0])
    def _():
        ext[:, 0:2, 0:own, :] = jnp.zeros_like(ext[:, 0:2, 0:own, :])
        fx_in[:, 0] = jnp.zeros_like(fx_in[:, 0])

    @pl.when(edges[1])
    def _():
        ext[:, own_x + 2 :, 0:own, :] = jnp.zeros_like(ext[:, own_x + 2 :, 0:own, :])
        fx_in[:, 1] = jnp.zeros_like(fx_in[:, 1])

    @pl.when(edges[2])
    def _():
        stage_in[0] = jnp.zeros_like(stage_in[0])
        fy_in[:, 0] = jnp.zeros_like(fy_in[:, 0])

    @pl.when(edges[3])
    def _():
        stage_in[1] = jnp.zeros_like(stage_in[1])
        fy_in[:, 1] = jnp.zeros_like(fy_in[:, 1])

    pl.semaphore_wait(barrier, devs - 1)
    x_halo[0]()
    stage(own_planes)
    y_halo[0]()

    def scatter(src, dst, s):
        def step(i, carry):
            peer = lax.rem(me + i, devs)
            pltpu.make_async_remote_copy(
                src.at[peer], dst.at[me], a2a_send.at[s], a2a_recv.at[s],
                device_id=(peer // n_grp, lax.rem(peer, n_grp)), device_id_type=MESH,
            ).start()
            return carry

        lax.fori_loop(1, devs, step, 0)
        dst[me] = src[me]

    def settle(src, dst, s):
        peer = lax.rem(me + 1, devs)
        return pltpu.make_async_remote_copy(
            src.at[0 : devs - 1], dst.at[0 : devs - 1], a2a_send.at[s], a2a_recv.at[s],
            device_id=(peer // n_grp, lax.rem(peer, n_grp)), device_id_type=MESH,
        )

    wide[...] = jnp.zeros_like(wide)
    for c in range(4):
        wide[c, 0:125, :] = state_ref[:, c, :]
    owned = jnp.concatenate([wide[c].T for c in range(4)], axis=1)
    by_place = slot_matrix(place_ref, devs, cap)
    out_buf[...] = spread(by_place, owned).reshape(out_buf.shape)
    scatter(out_buf, in_buf, 0)

    for load in loads:
        load.wait()
    order, reorder, own_mat, own_low, send_mat, take_mat = local
    proj_rows[...] = jnp.zeros_like(proj_rows)
    proj_rows[0:125, :] = mm(proj_ref[...], reorder[...])

    def send_faces(state, t):
        faces = faces_out(state, send_mat[...])
        fx_out[t, 0] = faces[:, 0:128].T[0:80]
        fx_out[t, 1] = faces[:, 128:256].T[0:80]
        fy_out[t, 0] = faces[:bz, 256:384]
        fy_out[t, 1] = faces[count - bz :, 384:512]
        x_face[t][0]()
        y_face[t][0]()
        return faces

    def face_rows(value):
        return jnp.concatenate([value, jnp.zeros((48, count), F32)], axis=0).T

    def take_faces(state, faces, source, t):
        base = state + own_change(state, own_mat[...], own_low[...]) - TIME_STEP_ACOUSTIC * source
        x_face[t][1]()
        y_face[t][1]()
        return advance(
            base, faces, face_rows(fx_in[t, 0]), face_rows(fx_in[t, 1]), fy_in[t, 0], fy_in[t, 1],
            take_mat[...], bz,
        )

    to_home = home_matrix(send_ref, count)
    y_halo[1]()
    unstage(own_planes)
    les_first(ext, mid, own, edges, ((2, own_x),))
    x_halo[1]()
    stage(end_planes)
    corners[0]()
    settle(out_buf, in_buf, 0).wait_recv()
    state = gather(to_home, in_buf[...].reshape(devs * 8, in_buf.shape[2]))
    faces = send_faces(state, 0)
    corners[1]()
    unstage(end_planes)
    les_first(ext, mid, own, edges, ((0, 2), (own_x, own_x + 2)))
    les_lamb(mid, cells, own)
    source = source_rows(cells, order[...], proj_rows[...].astype(BF16))
    leave = [m.T for m in to_home]
    for t in range(AC_SECTIONS):
        state = take_faces(state, faces, source, t)
        if t < AC_SECTIONS - 1:
            faces = send_faces(state, t + 1)

    back_out[...] = spread(leave, state).reshape(back_out.shape)
    scatter(back_out, back_in, 1)
    les_second(ext, mid, vel_out_ref)
    from_home = [m.T for m in by_place]
    settle(back_out, back_in, 1).wait_recv()
    final = gather(from_home, back_in[...].reshape(devs * 8, back_in.shape[2]))
    for c in range(4):
        out_ref[c] = final[:, 128 * c : 128 * (c + 1)].T

    settle(out_buf, in_buf, 0).wait_send()
    settle(back_out, back_in, 1).wait_send()
    x_halo[2]()
    y_halo[2]()
    corners[2]()
    for t in range(AC_SECTIONS):
        x_face[t][2]()
        y_face[t][2]()


def write_kernel(vel_ref, rows_ref, vel_out_ref, out_ref, sem):
    copy = pltpu.make_async_copy(vel_ref, vel_out_ref, sem)
    copy.start()
    for c in range(4):
        out_ref[:, c, :] = rows_ref[c, 0:125]
    copy.wait()


def body(velocity, eddy_visc, projection, acoustic_state, route_send, route_place):
    own_x, own_y, lanes = velocity.shape[1:]
    by, bz = own_y // 8, lanes // 8
    sizes = (lax.axis_size("flow"), lax.axis_size("grp"))
    cap = route_send.shape[2]
    count = acoustic_state.shape[2]
    devs = sizes[0] * sizes[1]
    width = 512 * cap // 8
    ids = np.arange(512)
    reorder = np.zeros((512, 512), ml_dtypes.bfloat16)
    reorder[ids, (ids % 8) * 64 + ids // 8] = 1
    consts = [jnp.asarray(m) for m in (cell_order(by, bz), reorder, *operators())]
    args = (
        velocity, eddy_visc, acoustic_state.transpose(1, 0, 2), route_place, route_send[0].T, projection
    )
    vmem = pl.BlockSpec(memory_space=pltpu.VMEM)
    dma = pltpu.SemaphoreType.DMA
    chunk = pltpu.VMEM((devs, 8, width), F32)
    vel_rows, final = pl.pallas_call(
        functools.partial(kernel, sizes, cap, bz),
        out_shape=[
            jax.ShapeDtypeStruct(velocity.shape, F32),
            jax.ShapeDtypeStruct((4, 128, count), F32),
        ],
        in_specs=[vmem] * len(args) + [pl.BlockSpec(memory_space=pl.ANY)] * len(consts),
        out_specs=[vmem] * 2,
        scratch_shapes=[pltpu.VMEM(c.shape, BF16) for c in consts] + [
            pltpu.VMEM((4, own_x + 4, own_y + 8, lanes), F32),
            pltpu.VMEM((3, own_x + 2, own_y + 8, lanes), F32),
            pltpu.VMEM((3, own_x * 8, by * lanes), F32),
            pltpu.VMEM((4, 128, count), F32),
            pltpu.VMEM((128, 512), F32),
            chunk, chunk, chunk, chunk,
            pltpu.VMEM((2, own_x + 4, 8, lanes), F32),
            pltpu.VMEM((2, own_x + 4, 8, lanes), F32),
            pltpu.VMEM((AC_SECTIONS, 2, 80, count), F32),
            pltpu.VMEM((AC_SECTIONS, 2, 80, count), F32),
            pltpu.VMEM((AC_SECTIONS, 2, bz, 128), F32),
            pltpu.VMEM((AC_SECTIONS, 2, bz, 128), F32),
            dma((len(consts),)), dma((2,)), dma((2,)), dma((6,)), dma((6,)),
            dma((AC_SECTIONS, 4)), dma((AC_SECTIONS, 4)),
        ],
        compiler_params=pltpu.CompilerParams(
            collective_id=0, has_side_effects=True, vmem_limit_bytes=56 * 2**20
        ),
    )(*args, *consts)
    vel_out, nodes = pl.pallas_call(
        write_kernel,
        out_shape=[
            jax.ShapeDtypeStruct(velocity.shape, F32),
            jax.ShapeDtypeStruct((125, 4, count), F32),
        ],
        in_specs=[vmem, vmem],
        out_specs=[pl.BlockSpec(memory_space=pl.ANY), vmem],
        scratch_shapes=[pltpu.SemaphoreType.DMA],
    )(vel_rows, final)
    return vel_out, nodes.transpose(1, 0, 2)


def solution(mesh):
    placed = (
        P(None, "flow", "grp", None),
        P("flow", "grp", None),
        P(),
        P(None, None, ("flow", "grp")),
        P(("flow", "grp"), None, None),
        P(("flow", "grp"), None),
    )
    return jax.shard_map(
        body,
        mesh=mesh,
        in_specs=placed,
        out_specs=(P(None, "flow", "grp", None), P(None, None, ("flow", "grp"))),
        check_vma=False,
    )
```
